256 devices in a mesh: pipe: 4 (over y), dp: 32 (over z, x), tensor: 2 (over core).
Axes of the slice: x: 4, y: 4, z: 8, core: 2. Of those that a mesh axis runs over, the one named last changes fastest.
Arguments:
- llm_grad: bfloat16 [4, 1024, 1664], P(None, 'dp'), may hold values from -6 to 6
- slot_row: int32 [4, 32, 32], P(None, 'dp'), may hold values from 0 to 31, each once within a row
- counts: int32 [32, 4], P('dp'), may hold values from 8 to 32, as said below
- saved_in: bfloat16 [4, 4, 1024, 1664], P('pipe', None, 'dp'), may hold values from -6 to 6
- saved_pre: bfloat16 [4, 4, 1024, 6400], P('pipe', None, 'dp', 'tensor'), may hold values from -6 to 6
- weights: bfloat16 [4, 1664, 6400], P('pipe', 'dp', 'tensor'), may hold values from -0.15625 to 0.15625
- channel_scale: float32 [4, 1664], P('pipe'), may hold values from 0.25 to 2
Outputs:
- weight_grad: bfloat16 [4, 1664, 6400], P('pipe', 'dp', 'tensor')
- section_grad: bfloat16 [4, 4, 1024, 1664], P('pipe', None, 'dp')
The draws below stay inside these ranges and needn't reach their ends.
Inputs may be any that keep to these rules, and one draw needn't show every extreme that they name: For each micro-batch and rank, slot_row lists every row of the rank once. `counts`: both ends of the range occur in every draw.
All inputs are finite; a program needn't handle non-finite values.
Results may differ from the reference program's by a relative error of at most 0.023.
Values may be sent and summed in bfloat16 or wider, within the bound.
A program may use at most 128 MiB of HBM per device.

```python
import math
import jax
import jax.numpy as jnp
from jax import lax

D = 1664
FF = 6400
ROWS = 32
MICRO = 4
SECTIONS = 4
RANKS = 32
TOKENS = 1024


def draw_counts(key, part):
    key_values, key_high, key_low = jax.random.split(key, 3)
    count_all = RANKS * MICRO
    values = jax.random.randint(key_values, (count_all,), ROWS // 4, ROWS + 1, dtype=jnp.int32)
    high_at = jax.random.randint(key_high, (), 0, count_all, dtype=jnp.int32)
    low_at = (high_at + 1 + jax.random.randint(key_low, (), 0, count_all - 1, dtype=jnp.int32)) % count_all
    places = jnp.arange(count_all, dtype=jnp.int32)
    values = jnp.where(places == high_at, ROWS, values)
    values = jnp.where(places == low_at, ROWS // 4, values)
    return values.reshape(RANKS, MICRO).astype(jnp.int32)


def steps_of(own_key, dims, cuts, smallest, largest):
    factor_of, own = 1.0, jax.random.fold_in(own_key, 6)
    for axis_at, parts in cuts:
        heights = jnp.exp(jax.random.uniform(jax.random.fold_in(own, axis_at), (parts,), jnp.float32, smallest / len(cuts), largest / len(cuts)))
        factor_of = factor_of * jnp.repeat(heights, dims[axis_at] // parts).reshape([-1 if axis == axis_at else 1 for axis in range(len(dims))])
    return factor_of


def centred(rng, extent, scale, reach, pieces=(), held_as=jnp.bfloat16):
    drawn = jax.random.normal(rng, extent, jnp.float32) * scale
    if len(pieces) > 0:
        drawn = steps_of(rng, extent, pieces, -0.22, 0.18) * drawn
    return jnp.clip(drawn, min=-reach, max=reach).astype(held_as)


def setup_inputs(seed: int = 0) -> dict:
    keys = jax.random.split(jax.random.key(seed), 8)
    return {
        "llm_grad": centred(keys[0], (MICRO, TOKENS, D), 1.0, 6.0, ((1, 32),)),
        "slot_row": jax.vmap(lambda own: jax.random.permutation(own, ROWS))(jax.random.split(keys[1], MICRO * RANKS)).reshape((MICRO, RANKS, ROWS)).astype(jnp.int32),
        "counts": draw_counts(jax.random.fold_in(keys[7], 71), 0),
        "saved_in": centred(keys[3], (SECTIONS, MICRO, TOKENS, D), 1.0, 6.0, ((0, 4), (2, 32))),
        "saved_pre": centred(keys[4], (SECTIONS, MICRO, TOKENS, FF), 1.0, 6.0, ((0, 4), (2, 32), (3, 2))),
        "weights": centred(keys[5], (SECTIONS, D, FF), D ** -0.5, 0.15625, ((0, 4), (1, 32), (2, 2))),
        "channel_scale": jnp.clip(jnp.exp(math.log(2.0) - 2.0794415 * jax.random.uniform(keys[6], (SECTIONS, D), jnp.float32) ** steps_of(keys[6], (SECTIONS, D), ((0, 4),), -0.2, 0.2)), 0.25, 2.0),
    }


norm_eps = 1e-06
root_half = 0.7071067811865476
inv_root_two_pi = 0.3989422804014327

def gelu_parts(pre_act):
    normal_cdf = 0.5 * (1.0 + jax.scipy.special.erf(pre_act * root_half))
    density = jnp.exp(-0.5 * pre_act * pre_act) * inv_root_two_pi
    return (pre_act * normal_cdf, normal_cdf + pre_act * density)

def top_gradient(llm_grad, slot_row, counts):
    slot_ids = jnp.arange(ROWS, dtype=jnp.int32)
    kept_mask = slot_ids[None, None, :] < jnp.transpose(counts)[:, :, None]
    source = llm_grad.reshape(MICRO, RANKS, ROWS, D).astype(jnp.float32)
    source = jnp.where(kept_mask[..., None], source, jnp.zeros_like(source))
    onehot = (slot_row[..., :, None] == slot_ids[None, None, None, :]).astype(jnp.float32)
    placed = jnp.einsum('abjr,abjd->abrd', onehot, source)
    return placed.reshape(MICRO, TOKENS, D).astype(jnp.bfloat16)

def rank_sum(left_side, right_side):
    left_ranks = left_side.reshape(MICRO, RANKS, ROWS, D)
    right_ranks = right_side.reshape(MICRO, RANKS, ROWS, FF)

    def add_rank(grad_total, rank_index):
        left_part = lax.dynamic_index_in_dim(left_ranks, rank_index, 1, keepdims=False).reshape(MICRO * ROWS, D)
        right_part = lax.dynamic_index_in_dim(right_ranks, rank_index, 1, keepdims=False).reshape(MICRO * ROWS, FF)
        term = jnp.dot(left_part.T, right_part, preferred_element_type=jnp.float32)
        rounded = lax.optimization_barrier(term.astype(jnp.bfloat16))
        return (grad_total + rounded.astype(jnp.float32), None)
    grad_total, unused = lax.scan(add_rank, jnp.zeros((D, FF), jnp.float32), jnp.arange(RANKS, dtype=jnp.int32))
    return grad_total.astype(jnp.bfloat16)

def reference(llm_grad, slot_row, counts, saved_in, saved_pre, weights, channel_scale):
    incoming = top_gradient(llm_grad, slot_row, counts)
    hidden_grad = None
    section_list = []
    weight_list = []
    for section_index in range(SECTIONS - 1, -1, -1):
        channel_gain = channel_scale[section_index]
        weight_now = weights[section_index]
        pre_act = saved_pre[section_index].astype(jnp.float32)
        if section_index % 2 == 1:
            scaled = (incoming.astype(jnp.float32) * channel_gain).astype(jnp.bfloat16)
            hidden_grad = jnp.dot(scaled.reshape(-1, D), weight_now, preferred_element_type=jnp.float32)
            hidden_grad = hidden_grad.reshape(MICRO, TOKENS, FF).astype(jnp.bfloat16)
            activated = gelu_parts(pre_act)[0].astype(jnp.bfloat16)
            outgoing = incoming
            left_side, right_side = (scaled, activated)
        else:
            act_grad = (hidden_grad.astype(jnp.float32) * gelu_parts(pre_act)[1]).astype(jnp.bfloat16)
            values = saved_in[section_index].astype(jnp.float32)
            center = values - lax.optimization_barrier(jnp.mean(values, axis=-1, keepdims=True))
            inv_std = lax.rsqrt(lax.optimization_barrier(jnp.mean(center * center, axis=-1, keepdims=True)) + norm_eps)
            unit_rows = center * inv_std
            normed = (unit_rows * channel_gain).astype(jnp.bfloat16)
            dnorm = jnp.dot(act_grad.reshape(-1, FF), weight_now.T, preferred_element_type=jnp.float32)
            scaled_back = dnorm.reshape(MICRO, TOKENS, D) * channel_gain
            back = inv_std * (scaled_back - lax.optimization_barrier(jnp.mean(scaled_back, axis=-1, keepdims=True)) - unit_rows * lax.optimization_barrier(jnp.mean(scaled_back * unit_rows, axis=-1, keepdims=True)))
            outgoing = (incoming.astype(jnp.float32) + back).astype(jnp.bfloat16)
            left_side, right_side = (normed, act_grad)
        section_list.append(outgoing)
        weight_list.append(rank_sum(left_side, right_side))
        incoming = outgoing
    section_grad = jnp.stack(section_list[::-1], axis=0)
    weight_grad = jnp.stack(weight_list[::-1], axis=0)
    return (weight_grad, section_grad)
```

```python
import functools

import jax
import jax.numpy as jnp
from jax import lax
from jax.experimental import pallas as pl
from jax.experimental.pallas import tpu as pltpu
from jax.sharding import PartitionSpec as P

norm_eps = 1e-06
root_half = 0.7071067811865476
inv_root_two_pi = 0.3989422804014327

MESH = pl.DeviceIdType.MESH
f32 = jnp.float32
bf16 = jnp.bfloat16

NX, NY, NZ = 4, 4, 8
GROUP = NX * NY
D = 1664
ROWS = 32
HALF = 16
TOK = 512
OWN = 52
PAD = 64
PACK = NX * OWN
LANE = 128
WIDE = 256
BLOCKS = 25
SECTIONS = 4


def first_block(piece):
    return (23 * piece) // 15


def gelu_value(p):
    return p * (0.5 * (1.0 + lax.erf(p * root_half)))


def gelu_slope(p):
    cdf = 0.5 * (1.0 + lax.erf(p * root_half))
    return cdf + p * (jnp.exp(-0.5 * p * p) * inv_root_two_pi)


def kernel(
    llm, slots, counts, xin, pre, w, scale,
    wout, gout,
    wx, wg, preb, full, scaled, part, sibs, sibr, rss, rsr, act, slope, agrad,
    dwp, zs, zr, outs, outr, scl, xi, g0f, g0s,
    local_sem, wx_s, wx_r, pre_s, pre_r, sc_s, sc_r, xi_s, xi_r,
    ag_s, ag_r, sib_s, sib_r, cs_s, cs_r, rs_s, rs_r,
    zag_s, zag_r, zrs_s, zrs_r, out_s, out_r, g0_s, g0_r, g1_s, g1_r,
):
    y = lax.axis_index("pipe")
    dp = lax.axis_index("dp")
    c = lax.axis_index("tensor")
    z = lax.div(dp, NX)
    x = lax.rem(dp, NX)
    gid = x * NY + y
    oc = 1 - c
    sibling = (y, dp, oc)
    up_z = (y, lax.rem(z + 1, NZ) * NX + x, c)
    down_z = (y, lax.rem(z + NZ - 1, NZ) * NX + x, c)

    def place(piece):
        return (lax.rem(piece, NY), z * NX + lax.div(piece, NY), c)

    def other(k):
        return lax.rem(gid + k, GROUP)

    def loop(low, high, body):
        def step(k, carry):
            body(k)
            return carry

        lax.fori_loop(low, high, step, 0)

    def remote(src, dst, send, recv, where):
        return pltpu.make_async_remote_copy(
            src_ref=src, dst_ref=dst, send_sem=send, recv_sem=recv, device_id=where, device_id_type=MESH
        )

    def take(ref, sem):
        pltpu.make_async_copy(ref, ref, sem).wait()

    def columns(piece):
        return pl.ds(pl.multiple_of(lax.div(23 * piece, 15) * LANE, LANE), WIDE)

    barrier = pltpu.get_barrier_semaphore()

    def greet(k):
        pl.semaphore_signal(barrier, inc=1, device_id=place(other(k)), device_id_type=MESH)

    loop(1, GROUP, greet)
    for where in (sibling, up_z, down_z):
        pl.semaphore_signal(barrier, inc=1, device_id=where, device_id_type=MESH)
    pl.semaphore_wait(barrier, GROUP + 2)

    own_w = pltpu.make_async_copy(w.at[:, columns(gid)], wx.at[y * NX + x], local_sem.at[0])
    own_w.start()
    own_pre = pltpu.make_async_copy(pre.at[:, columns(gid)], preb.at[y * NX + x], local_sem.at[1])
    own_pre.start()

    def send_w(k):
        p = other(k)
        remote(w.at[:, columns(p)], wx.at[y * NX + x], wx_s, wx_r, place(p)).start()

    loop(1, GROUP, send_w)

    scl[y] = scale[...]

    def send_scale(k):
        py = lax.rem(y + k, NY)
        remote(scale, scl.at[y], sc_s, sc_r, (py, dp, c)).start()

    loop(1, NY, send_scale)

    slot_line = slots[pl.ds(y, 1), :]
    row_ids = lax.broadcasted_iota(jnp.int32, (HALF, ROWS), 0) + c * HALF
    slot_ids = lax.broadcasted_iota(jnp.int32, (HALF, ROWS), 1)
    hit = (slot_line == row_ids) & (slot_ids < counts[0, y])
    onehot = jnp.where(hit, 1.0, 0.0).astype(bf16)
    full[0, gid, c] = jnp.dot(onehot, llm[y], preferred_element_type=f32).astype(bf16)

    def ag_send(i):
        def send(k):
            mine = full.at[i, gid, c]
            remote(mine, mine, ag_s.at[i], ag_r.at[i], place(other(k))).start()

        loop(1, GROUP, send)

    def ag_forward(i):
        take(full.at[i, pl.ds(0, GROUP - 1), 0], ag_r.at[i])
        half = full.at[i, :, c]
        remote(half, half, sib_s.at[i], sib_r.at[i], sibling).start()

    def ag_finish(i):
        take(full.at[i, :, oc], sib_r.at[i])

    ag_send(0)

    def send_pre(k):
        p = other(k)
        remote(pre.at[:, columns(p)], preb.at[y * NX + x], pre_s, pre_r, place(p)).start()

    loop(1, GROUP, send_pre)

    half_rows = pl.ds(pl.multiple_of(c * HALF, HALF), HALF)
    for b, s in ((0, 2), (1, 0)):

        @pl.when(y == s)
        def _():
            xi[b] = xin[y, half_rows, :]

            def send(k):
                py = lax.rem(y + k, NY)
                remote(xin.at[py, half_rows, :], xi.at[b], xi_s.at[b], xi_r.at[b], (py, dp, c)).start()

            loop(1, NY, send)

    take(wx.at[pl.ds(0, GROUP - 1)], wx_r)
    own_w.wait()
    to_row = lax.broadcasted_iota(jnp.int32, (PACK, NX * PAD), 0)
    from_row = lax.broadcasted_iota(jnp.int32, (PACK, NX * PAD), 1)
    from_block = lax.shift_right_logical(from_row, 6)
    inside = from_row - from_block * PAD
    picks = (inside < OWN) & (from_block * OWN + inside == to_row)
    pick = jnp.where(picks, 1.0, 0.0).astype(bf16)

    def pack(s):
        blocks = wx[s * NX : (s + 1) * NX].reshape(NX * PAD, WIDE)
        wg[s, z] = jnp.dot(pick, blocks, preferred_element_type=f32).astype(bf16)

    def zag_block(s, chunk, d, k):
        if k == 4:
            return wg.at[s, chunk, :, pl.ds(d * LANE, LANE)]
        return wg.at[s, chunk]

    def zag_take(s, k):
        for d, chunk in ((0, lax.rem(z - k + NZ, NZ)), (1, lax.rem(z + k, NZ))):
            take(zag_block(s, chunk, d, k), zag_r.at[s, d, k - 1])

    def zag(s, k):
        if k > 1:
            zag_take(s, k - 1)
        for d, chunk, where in (
            (0, lax.rem(z - k + 1 + NZ, NZ), up_z),
            (1, lax.rem(z + k - 1, NZ), down_z),
        ):
            block = zag_block(s, chunk, d, k)
            remote(block, block, zag_s.at[s, d, k - 1], zag_r.at[s, d, k - 1], where).start()

    def zrs(s, k):
        ways = ((0, lax.rem(z + 5 - k + NZ, NZ), up_z), (1, lax.rem(z - 5 + k + NZ, NZ), down_z))
        for d, chunk, where in ways:
            rows = pl.ds(pl.multiple_of(chunk * PACK, HALF), PACK)
            side = pl.ds(d * LANE, LANE)
            if k == 1:
                zs[s, d, 0, :, side] = dwp[s, rows, side].astype(bf16)
                src, dst = zs.at[s, d, 0, :, side], zr.at[s, d, 0, :, side]
            else:
                if k == 2:
                    take(zr.at[s, d, 0, :, side], zrs_r.at[s, d, 0])
                    there = pl.ds((1 - d) * LANE, LANE)
                    zs[s, d, 1, :, side] = (dwp[s, rows, side] + zr[s, d, 0, :, side].astype(f32)).astype(bf16)
                    zs[s, d, 1, :, there] = dwp[s, rows, there].astype(bf16)
                else:
                    take(zr.at[s, d, k - 2], zrs_r.at[s, d, k - 2])
                    zs[s, d, k - 1] = (dwp[s, rows, :] + zr[s, d, k - 2].astype(f32)).astype(bf16)
                src, dst = zs.at[s, d, k - 1], zr.at[s, d, k - 1]
            remote(src, dst, zrs_s.at[s, d, k - 1], zrs_r.at[s, d, k - 1], where).start()

    def zrs_finish(s):
        for d in range(2):
            take(zr.at[s, d, 3], zrs_r.at[s, d, 3])
        rows = pl.ds(pl.multiple_of(z * PACK, HALF), PACK)
        total = dwp[s, rows, :] + zr[s, 0, 3].astype(f32) + zr[s, 1, 3].astype(f32)
        spread = lax.dot_general(pick, total.astype(bf16), (((0,), (0,)), ((), ())), preferred_element_type=f32)
        outs[s * NX : (s + 1) * NX] = spread.astype(bf16).reshape(NX, PAD, WIDE)

        def send(px):
            mine = (y == s) & (px == x)

            @pl.when(mine)
            def _():
                outr[gid] = outs[s * NX + px]

            @pl.when(jnp.logical_not(mine))
            def _():
                remote(outs.at[s * NX + px], outr.at[gid], out_s, out_r, (s, z * NX + px, c)).start()

        loop(0, NX, send)

    pack(3)
    zag(3, 1)
    pack(2)
    zag(2, 1)
    pack(1)
    pack(0)

    take(scl.at[pl.ds(0, NY - 1)], sc_r)

    def unit_rows(b):
        values = xi[b].astype(f32)
        center = values - jnp.mean(values, axis=-1, keepdims=True)
        inv_std = lax.rsqrt(jnp.mean(center * center, axis=-1, keepdims=True) + norm_eps)
        return center * inv_std, inv_std

    for b, s in ((0, 2), (1, 0)):

        @pl.when(y != s)
        def _():
            take(xi.at[b], xi_r.at[b])

        unit, inv_std = unit_rows(b)
        full[1 + 2 * b, gid, c] = (unit * scl[s]).astype(bf16)

    ag_send(1)
    zag(3, 2)
    zag(2, 2)
    ag_forward(0)
    zag(3, 3)
    zag(2, 3)

    def scale_rows(i, s):
        def one(p):
            rows = full[2 * i, p].astype(f32) * scl[s]
            scaled[i, p] = rows.astype(bf16)

        loop(0, GROUP, one)

    ag_finish(0)
    scale_rows(0, 3)
    zag(3, 4)
    zag(2, 4)

    def gelu_rows(b, down, up):
        def one(p):
            rows = pl.ds(pl.multiple_of(lax.rem(p, NY) * ROWS, ROWS), ROWS)
            at = pl.ds(pl.multiple_of(p * ROWS, ROWS), ROWS)
            act[b, at, :] = gelu_value(preb[down * NX + lax.div(p, NY), rows, :].astype(f32)).astype(bf16)
            slope[b, at, :] = gelu_slope(preb[up * NX + lax.div(p, NY), rows, :].astype(f32))

        loop(0, GROUP, one)

    take(preb.at[pl.ds(0, GROUP - 1)], pre_r)
    own_pre.wait()
    gelu_rows(0, 3, 2)

    repeated = jnp.where((lax.rem(gid, 2) == 1) & (gid < 14), LANE, 0)
    keep = lax.broadcasted_iota(jnp.int32, (WIDE, WIDE), 1) >= repeated

    def hidden_back(b, down):
        weight = wg[down].reshape(D, WIDE)
        for t in range(2):
            left = scaled[b, t * 8 : t * 8 + 8].reshape(WIDE, D)
            hidden = jnp.dot(left, weight, preferred_element_type=f32).astype(bf16).astype(f32)
            at = pl.ds(t * WIDE, WIDE)
            agrad[b, at, :] = (hidden * slope[b, at, :]).astype(bf16)

    def norm_part(b, up):
        weight = wg[up].reshape(D, WIDE)
        for t in range(2):
            rows = agrad[b, pl.ds(t * WIDE, WIDE), :]
            rows = jnp.where(keep, rows, jnp.zeros_like(rows))
            product = lax.dot_general(rows, weight, (((1,), (1,)), ((), ())), preferred_element_type=f32)
            part[t * 8 : t * 8 + 8] = product.reshape(8, 2, HALF, D)

    def rs_start(b):
        def one(p):
            sibs[b, p] = part[p, oc].astype(bf16)

        loop(0, GROUP, one)
        remote(sibs.at[b], sibr.at[b], cs_s.at[b], cs_r.at[b], sibling).start()

    def rs_middle(b):
        take(sibr.at[b], cs_r.at[b])

        def one(k):
            p = other(k)
            rss[b, p] = (part[p, c] + sibr[b, p].astype(f32)).astype(bf16)
            remote(rss.at[b, p], rsr.at[b, gid], rs_s.at[b], rs_r.at[b], place(p)).start()

        loop(1, GROUP, one)

    def rs_finish(b, s):
        take(rsr.at[b, pl.ds(0, GROUP - 1)], rs_r.at[b])
        total = part[gid, c] + sibr[b, gid].astype(f32)

        def add(k, so_far):
            return so_far + rsr[b, other(k)].astype(f32)

        total = lax.fori_loop(1, GROUP, add, total)
        unit, inv_std = unit_rows(b)
        back = total * scl[s]
        back = inv_std * (
            back
            - jnp.mean(back, axis=-1, keepdims=True)
            - unit * jnp.mean(back * unit, axis=-1, keepdims=True)
        )
        return (full[2 * b, gid, c].astype(f32) + back).astype(bf16)

    def weight_part(s, left_ref, right):
        for low, size in ((0, 512), (512, 512), (1024, 640)):
            left = left_ref[:, :, :, low : low + size].reshape(TOK, size)
            dwp[s, low : low + size, :] = lax.dot_general(
                left, right, (((0,), (0,)), ((), ())), preferred_element_type=f32
            )

    zag_take(3, 4)
    hidden_back(0, 3)
    zag(1, 1)
    zag(0, 1)
    zag_take(2, 4)
    norm_part(0, 2)
    rs_start(0)
    zag(1, 2)
    zag(0, 2)
    weight_part(3, scaled.at[0], act[0])
    rs_middle(0)
    zrs(3, 1)
    ag_forward(1)
    zag(1, 3)
    zag(0, 3)
    gelu_rows(1, 1, 0)
    full[2, gid, c] = rs_finish(0, 2)
    ag_send(2)
    zag(1, 4)
    zag(0, 4)
    ag_finish(1)
    weight_part(2, full.at[1], agrad[0])
    zrs(2, 1)
    zrs(3, 2)
    ag_send(3)
    ag_forward(2)
    zrs(3, 3)
    zrs(2, 2)
    ag_finish(2)
    scale_rows(1, 1)
    zag_take(1, 4)
    hidden_back(1, 1)
    zag_take(0, 4)
    norm_part(1, 0)
    rs_start(1)
    weight_part(1, scaled.at[1], act[1])
    zrs(1, 1)
    zrs(3, 4)
    zrs(2, 3)
    rs_middle(1)
    ag_forward(3)
    ag_finish(3)
    weight_part(0, full.at[3], agrad[1])
    zrs(0, 1)
    zrs(2, 4)
    zrs(1, 2)
    zrs(0, 2)
    zrs_finish(3)
    zrs(1, 3)
    zrs(0, 3)
    last = rs_finish(1, 0)

    @pl.when(y == 0)
    def _():
        g0f[0, c] = last

    @pl.when(y != 0)
    def _():
        g0s[...] = last
        remote(g0s, g0f.at[y, c], g0_s, g0_r, (0, dp, c)).start()

    zrs_finish(2)
    zrs(1, 4)
    zrs(0, 4)
    zrs_finish(1)
    zrs_finish(0)

    @pl.when(y == 0)
    def _():
        take(g0f.at[pl.ds(1, NY - 1), 0], g0_r)
        half = g0f.at[:, c]
        remote(half, half, g1_s, g1_r, sibling).start()
        take(g0f.at[:, oc], g1_r)
        gout[...] = g0f[...].reshape(NY * ROWS, D)
        take(half, g1_s)

    own = pl.ds(x * NY, NY)

    @pl.when((y == 1) | (y == 2))
    def _():
        gout[...] = full[2, own].reshape(NY * ROWS, D)

    @pl.when(y == 3)
    def _():
        gout[...] = full[0, own].reshape(NY * ROWS, D)

    take(outr.at[pl.ds(0, GROUP - 1)], out_r)
    for p in range(GROUP):
        low = first_block(p) * LANE
        wout[:, low : low + WIDE] = outr[p]

    take(wx.at[pl.ds(0, GROUP - 1)], wx_s)
    take(preb.at[pl.ds(0, GROUP - 1)], pre_s)
    take(scl.at[pl.ds(0, NY - 1)], sc_s)
    for b, s in ((0, 2), (1, 0)):

        @pl.when(y == s)
        def _():
            take(full.at[0, pl.ds(0, NY - 1), 0], xi_s.at[b])

    for i in range(4):
        take(full.at[i, pl.ds(0, GROUP - 1), 0], ag_s.at[i])
        take(full.at[i, :, c], sib_s.at[i])
    for b in range(2):
        take(sibs.at[b], cs_s.at[b])
        take(rss.at[b, pl.ds(0, GROUP - 1)], rs_s.at[b])
    for s in range(SECTIONS):
        for d in range(2):
            for k in range(1, 5):
                take(zag_block(s, 0, d, k), zag_s.at[s, d, k - 1])
                if k == 1:
                    take(zs.at[s, d, 0, :, pl.ds(d * LANE, LANE)], zrs_s.at[s, d, 0])
                else:
                    take(zs.at[s, d, k - 1], zrs_s.at[s, d, k - 1])
    take(outs.at[pl.ds(0, GROUP - 1)], out_s)

    @pl.when(y != 0)
    def _():
        take(g0s, g0_s)


def body(llm_grad, slot_row, counts, saved_in, saved_pre, weights, channel_scale):
    hidden = saved_pre.shape[3]
    padded = jnp.pad(weights[0], ((0, PAD - OWN), (0, 0)))
    pre = saved_pre.reshape(NY * ROWS, hidden)
    vmem = pl.BlockSpec(memory_space=pltpu.VMEM)
    anywhere = pl.BlockSpec(memory_space=pl.ANY)
    dma = pltpu.SemaphoreType.DMA
    scratch = [
        pltpu.VMEM((GROUP, PAD, WIDE), bf16),
        pltpu.VMEM((SECTIONS, NZ, PACK, WIDE), bf16),
        pltpu.VMEM((GROUP, NY * ROWS, WIDE), bf16),
        pltpu.VMEM((4, GROUP, 2, HALF, D), bf16),
        pltpu.VMEM((2, GROUP, 2, HALF, D), bf16),
        pltpu.VMEM((GROUP, 2, HALF, D), f32),
        pltpu.VMEM((2, GROUP, HALF, D), bf16),
        pltpu.VMEM((2, GROUP, HALF, D), bf16),
        pltpu.VMEM((2, GROUP, HALF, D), bf16),
        pltpu.VMEM((2, GROUP, HALF, D), bf16),
        pltpu.VMEM((2, TOK, WIDE), bf16),
        pltpu.VMEM((2, TOK, WIDE), f32),
        pltpu.VMEM((2, TOK, WIDE), bf16),
        pltpu.VMEM((SECTIONS, D, WIDE), f32),
        pltpu.VMEM((SECTIONS, 2, 4, PACK, WIDE), bf16),
        pltpu.VMEM((SECTIONS, 2, 4, PACK, WIDE), bf16),
        pltpu.VMEM((GROUP, PAD, WIDE), bf16),
        pltpu.VMEM((GROUP, PAD, WIDE), bf16),
        pltpu.VMEM((SECTIONS, 1, D), f32),
        pltpu.VMEM((2, HALF, D), bf16),
        pltpu.VMEM((NY, 2, HALF, D), bf16),
        pltpu.VMEM((HALF, D), bf16),
        dma((2,)), dma, dma, dma, dma, dma, dma, dma((2,)), dma((2,)),
        dma((4,)), dma((4,)), dma((4,)), dma((4,)), dma((2,)), dma((2,)), dma((2,)), dma((2,)),
        dma((4, 2, 4)), dma((4, 2, 4)), dma((4, 2, 4)), dma((4, 2, 4)), dma, dma, dma, dma, dma, dma,
    ]
    wout, gout = pl.pallas_call(
        kernel,
        out_shape=(
            jax.ShapeDtypeStruct((PAD, hidden), bf16),
            jax.ShapeDtypeStruct((NY * ROWS, D), bf16),
        ),
        in_specs=[vmem, vmem, pl.BlockSpec(memory_space=pltpu.SMEM), vmem, anywhere, anywhere, vmem],
        out_specs=(vmem, vmem),
        scratch_shapes=scratch,
        compiler_params=pltpu.CompilerParams(
            collective_id=0, has_side_effects=True, vmem_limit_bytes=60 * 1024 * 1024
        ),
    )(llm_grad, slot_row[:, 0], counts, saved_in[0], pre, padded, channel_scale)
    return (wout[None, :OWN], gout.reshape(1, NY, ROWS, D))


def solution(mesh):
    in_specs = (
        P(None, "dp", None),
        P(None, "dp", None),
        P("dp", None),
        P("pipe", None, "dp", None),
        P("pipe", None, "dp", "tensor"),
        P("pipe", "dp", "tensor"),
        P("pipe", None),
    )
    out_specs = (P("pipe", "dp", "tensor"), P("pipe", None, "dp", None))
    return jax.shard_map(body, mesh=mesh, in_specs=in_specs, out_specs=out_specs, check_vma=False)
```

```python
import functools

import jax
import jax.numpy as jnp
from jax import lax
from jax.experimental import pallas as pl
from jax.experimental.pallas import tpu as pltpu
from jax.sharding import PartitionSpec as P

norm_eps = 1e-06
root_half = 0.7071067811865476
inv_root_two_pi = 0.3989422804014327

MESH = pl.DeviceIdType.MESH
f32 = jnp.float32
bf16 = jnp.bfloat16

NX, NY, NZ = 4, 4, 8
GROUP = NX * NY
D = 1664
ROWS = 32
HALF = 16
TOK = 512
OWN = 52
PAD = 64
PACK = NX * OWN
LANE = 128
WIDE = 256
BLOCKS = 25
SECTIONS = 4


def first_block(piece):
    return (23 * piece) // 15


def gelu_value(p):
    return p * (0.5 * (1.0 + lax.erf(p * root_half)))


def gelu_slope(p):
    cdf = 0.5 * (1.0 + lax.erf(p * root_half))
    return cdf + p * (jnp.exp(-0.5 * p * p) * inv_root_two_pi)


def kernel(
    llm, slots, counts, xin, pre, w, scale,
    wout, gout,
    wpad, wx, wg, preb, full, scaled, part, sibs, sibr, rss, rsr, act, slope, agrad,
    dwp, zs, zr, outs, outr, scl, xi, g0f, g0s,
    local_sem, wx_s, wx_r, pre_s, pre_r, sc_s, sc_r, xi_s, xi_r,
    ag_s, ag_r, far_s, far_r, sib_s, sib_r, cs_s, cs_r, rs_s, rs_r,
    zag_s, zag_r, zrs_s, zrs_r, out_s, out_r, g0_s, g0_r, g1_s, g1_r,
):
    y = lax.axis_index("pipe")
    dp = lax.axis_index("dp")
    c = lax.axis_index("tensor")
    z = lax.div(dp, NX)
    x = lax.rem(dp, NX)
    gid = x * NY + y
    oc = 1 - c
    sibling = (y, dp, oc)
    up_z = (y, lax.rem(z + 1, NZ) * NX + x, c)
    down_z = (y, lax.rem(z + NZ - 1, NZ) * NX + x, c)

    def place(piece):
        return (lax.rem(piece, NY), z * NX + lax.div(piece, NY), c)

    def other(k):
        return lax.rem(gid + k, GROUP)

    def loop(low, high, body):
        def step(k, carry):
            body(k)
            return carry

        lax.fori_loop(low, high, step, 0)

    def remote(src, dst, send, recv, where):
        return pltpu.make_async_remote_copy(
            src_ref=src, dst_ref=dst, send_sem=send, recv_sem=recv, device_id=where, device_id_type=MESH
        )

    def take(ref, sem):
        pltpu.make_async_copy(ref, ref, sem).wait()

    def columns(piece):
        return pl.ds(pl.multiple_of(lax.div(23 * piece, 15) * LANE, LANE), WIDE)

    barrier = pltpu.get_barrier_semaphore()

    def greet(k):
        pl.semaphore_signal(barrier, inc=1, device_id=place(other(k)), device_id_type=MESH)

    loop(1, GROUP, greet)
    for where in (sibling, up_z, down_z):
        pl.semaphore_signal(barrier, inc=1, device_id=where, device_id_type=MESH)
    own_pre = pltpu.make_async_copy(pre.at[:, columns(gid)], preb.at[y * NX + x], local_sem.at[1])
    own_pre.start()
    wpad[:OWN, :] = w[...]
    wpad[OWN:, :] = jnp.zeros((PAD - OWN, BLOCKS * LANE), bf16)
    own_w = pltpu.make_async_copy(wpad.at[:, columns(gid)], wx.at[y * NX + x], local_sem.at[0])
    own_w.start()
    scl[y] = scale[...]
    half_rows = pl.ds(pl.multiple_of(c * HALF, HALF), HALF)
    row_ids = lax.broadcasted_iota(jnp.int32, (HALF, ROWS), 0) + c * HALF
    slot_ids = lax.broadcasted_iota(jnp.int32, (HALF, ROWS), 1)
    for m in range(NY):
        hit = (slots[m : m + 1, :] == row_ids) & (slot_ids < counts[0, m])
        onehot = jnp.where(hit, 1.0, 0.0).astype(bf16)
        full[0, x, m, c] = jnp.dot(onehot, llm[m], preferred_element_type=f32).astype(bf16)
    for b, s in ((0, 2), (1, 0)):

        @pl.when(y == s)
        def _():
            xi[b] = xin[y, half_rows, :]

    pl.semaphore_wait(barrier, GROUP + 2)

    def send_w(k):
        p = other(k)
        remote(wpad.at[:, columns(p)], wx.at[y * NX + x], wx_s, wx_r, place(p)).start()

    loop(1, GROUP, send_w)

    def send_scale(k):
        py = lax.rem(y + k, NY)
        remote(scale, scl.at[y], sc_s, sc_r, (py, dp, c)).start()

    loop(1, NY, send_scale)

    def near(k):
        return lax.rem(x + k * (1 - c), NX), lax.rem(y + k * c, NY)

    def far(k):
        return lax.rem(x + k * c, NX), lax.rem(y + k * (1 - c), NY)

    def spread(i, q):
        px, py = near(q)
        piece = full.at[i, px, py, c]

        def send(k):
            fx, fy = far(k)
            remote(piece, piece, far_s.at[i, k], far_r.at[i, NX - k], (fy, z * NX + fx, c)).start()

        loop(1, NX, send)

    def ag_send(i):
        piece = full.at[i, x, y, c]

        def send(k):
            px, py = near(k)
            remote(piece, piece, ag_s.at[i, k], ag_r.at[i, NX - k], (py, z * NX + px, c)).start()

        loop(1, NX, send)
        spread(i, 0)

    def ag_spread(i):
        for q in (1, 3, 2):
            take(full.at[i, 0, 0, 0], ag_r.at[i, q])
            spread(i, q)
        give(i, 0)

    def give(i, k):
        fx, fy = far(k)

        @pl.when(c == 0)
        def _():
            four = full.at[i, :, fy, 0]
            remote(four, four, sib_s.at[i, k], sib_r.at[i, k], sibling).start()

        @pl.when(c == 1)
        def _():
            four = full.at[i, fx, :, 1]
            remote(four, four, sib_s.at[i, k], sib_r.at[i, k], sibling).start()

    def ag_forward(i):
        for k in (1, 3, 2):
            take(full.at[i, 0, :, 0], far_r.at[i, k])
            give(i, k)

    def ag_finish(i):
        for k in range(NX):
            take(full.at[i, 0, :, 0], sib_r.at[i, k])

    def top_send():
        @pl.when(c == 0)
        def _():
            piece = full.at[0, x, y, 0]

            def send(k):
                px, py = near(k)
                remote(piece, piece, ag_s.at[0, k], ag_r.at[0, NX - k], (py, z * NX + px, c)).start()

            loop(1, NX, send)

        @pl.when(c == 1)
        def _():
            four = full.at[0, x, :, 1]

            def send(k):
                fx, fy = far(k)
                remote(four, four, far_s.at[0, k], far_r.at[0, NX - k], (fy, z * NX + fx, c)).start()

            loop(1, NX, send)
            give(0, 0)

    def top_spread():
        @pl.when(c == 0)
        def _():
            for q in (1, 3, 2):
                take(full.at[0, 0, 0, 0], ag_r.at[0, q])
                spread(0, q)
            give(0, 0)

    def top_forward():
        for k in (1, 3, 2):

            @pl.when(c == 0)
            def _():
                take(full.at[0, 0, pl.ds(0, 3), 0], far_r.at[0, k])

            @pl.when(c == 1)
            def _():
                take(full.at[0, 0, :, 0], far_r.at[0, k])

            give(0, k)

    top_send()

    def send_pre(k):
        p = other(k)
        remote(pre.at[:, columns(p)], preb.at[y * NX + x], pre_s, pre_r, place(p)).start()

    for b, s in ((0, 2), (1, 0)):

        @pl.when(y == s)
        def _():
            def send(k):
                py = lax.rem(y + k, NY)
                remote(xin.at[py, half_rows, :], xi.at[b], xi_s.at[b], xi_r.at[b], (py, dp, c)).start()

            loop(1, NY, send)

    take(wx.at[pl.ds(0, GROUP - 1)], wx_r)
    own_w.wait()
    to_row = lax.broadcasted_iota(jnp.int32, (PACK, NX * PAD), 0)
    from_row = lax.broadcasted_iota(jnp.int32, (PACK, NX * PAD), 1)
    from_block = lax.shift_right_logical(from_row, 6)
    inside = from_row - from_block * PAD
    picks = (inside < OWN) & (from_block * OWN + inside == to_row)
    pick = jnp.where(picks, 1.0, 0.0).astype(bf16)

    def pack(s):
        blocks = wx[s * NX : (s + 1) * NX].reshape(NX * PAD, WIDE)
        wg[s, z] = jnp.dot(pick, blocks, preferred_element_type=f32).astype(bf16)

    def zag_block(s, chunk, d, k):
        if k == 4:
            return wg.at[s, chunk, :, pl.ds(d * LANE, LANE)]
        return wg.at[s, chunk]

    def zag_take(s, k):
        for d, chunk in ((0, lax.rem(z - k + NZ, NZ)), (1, lax.rem(z + k, NZ))):
            take(zag_block(s, chunk, d, k), zag_r.at[s, d, k - 1])

    def zag(s, k):
        if k > 1:
            zag_take(s, k - 1)
        for d, chunk, where in (
            (0, lax.rem(z - k + 1 + NZ, NZ), up_z),
            (1, lax.rem(z + k - 1, NZ), down_z),
        ):
            block = zag_block(s, chunk, d, k)
            remote(block, block, zag_s.at[s, d, k - 1], zag_r.at[s, d, k - 1], where).start()

    def zrs(s, k):
        ways = ((0, lax.rem(z + 5 - k + NZ, NZ), up_z), (1, lax.rem(z - 5 + k + NZ, NZ), down_z))
        for d, chunk, where in ways:
            rows = pl.ds(pl.multiple_of(chunk * PACK, HALF), PACK)
            side = pl.ds(d * LANE, LANE)
            if k == 1:
                zs[s, d, 0, :, side] = dwp[s, rows, side].astype(bf16)
                src, dst = zs.at[s, d, 0, :, side], zr.at[s, d, 0, :, side]
            else:
                if k == 2:
                    take(zr.at[s, d, 0, :, side], zrs_r.at[s, d, 0])
                    there = pl.ds((1 - d) * LANE, LANE)
                    zs[s, d, 1, :, side] = (dwp[s, rows, side] + zr[s, d, 0, :, side].astype(f32)).astype(bf16)
                    zs[s, d, 1, :, there] = dwp[s, rows, there].astype(bf16)
                else:
                    take(zr.at[s, d, k - 2], zrs_r.at[s, d, k - 2])
                    zs[s, d, k - 1] = (dwp[s, rows, :] + zr[s, d, k - 2].astype(f32)).astype(bf16)
                src, dst = zs.at[s, d, k - 1], zr.at[s, d, k - 1]
            remote(src, dst, zrs_s.at[s, d, k - 1], zrs_r.at[s, d, k - 1], where).start()

    def zrs_finish(s):
        for d in range(2):
            take(zr.at[s, d, 3], zrs_r.at[s, d, 3])
        rows = pl.ds(pl.multiple_of(z * PACK, HALF), PACK)
        total = dwp[s, rows, :] + zr[s, 0, 3].astype(f32) + zr[s, 1, 3].astype(f32)
        spread = lax.dot_general(pick, total.astype(bf16), (((0,), (0,)), ((), ())), preferred_element_type=f32)
        outs[s * NX : (s + 1) * NX] = spread.astype(bf16).reshape(NX, PAD, WIDE)

        def send(px):
            mine = (y == s) & (px == x)

            @pl.when(mine)
            def _():
                outr[gid] = outs[s * NX + px]

            @pl.when(jnp.logical_not(mine))
            def _():
                remote(outs.at[s * NX + px], outr.at[gid], out_s, out_r, (s, z * NX + px, c)).start()

        loop(0, NX, send)

    pack(3)
    zag(3, 1)
    pack(2)
    zag(2, 1)
    top_spread()
    loop(1, GROUP, send_pre)
    pack(1)
    pack(0)

    take(scl.at[pl.ds(0, NY - 1)], sc_r)

    def unit_rows(b):
        values = xi[b].astype(f32)
        center = values - jnp.mean(values, axis=-1, keepdims=True)
        inv_std = lax.rsqrt(jnp.mean(center * center, axis=-1, keepdims=True) + norm_eps)
        return center * inv_std, inv_std

    for b, s in ((0, 2), (1, 0)):

        @pl.when(y != s)
        def _():
            take(xi.at[b], xi_r.at[b])

        unit, inv_std = unit_rows(b)
        full[1 + 2 * b, x, y, c] = (unit * scl[s]).astype(bf16)

    ag_send(1)
    zag(3, 2)
    zag(2, 2)
    top_forward()
    zag(3, 3)
    zag(2, 3)

    def scale_rows(i, s):
        def one(p):
            rows = full[2 * i, lax.div(p, NY), lax.rem(p, NY)].astype(f32) * scl[s]
            scaled[i, p] = rows.astype(bf16)

        loop(0, GROUP, one)

    ag_finish(0)
    scale_rows(0, 3)
    zag(3, 4)
    zag(2, 4)

    def gelu_rows(b, down, up):
        def one(p):
            rows = pl.ds(pl.multiple_of(lax.rem(p, NY) * ROWS, ROWS), ROWS)
            at = pl.ds(pl.multiple_of(p * ROWS, ROWS), ROWS)
            act[b, at, :] = gelu_value(preb[down * NX + lax.div(p, NY), rows, :].astype(f32)).astype(bf16)
            slope[b, at, :] = gelu_slope(preb[up * NX + lax.div(p, NY), rows, :].astype(f32))

        loop(0, GROUP, one)

    take(preb.at[pl.ds(0, GROUP - 1)], pre_r)
    own_pre.wait()
    gelu_rows(0, 3, 2)

    repeated = jnp.where((lax.rem(gid, 2) == 1) & (gid < 14), LANE, 0)
    keep = lax.broadcasted_iota(jnp.int32, (WIDE, WIDE), 1) >= repeated

    def hidden_back(b, down):
        weight = wg[down].reshape(D, WIDE)
        for t in range(2):
            left = scaled[b, t * 8 : t * 8 + 8].reshape(WIDE, D)
            hidden = jnp.dot(left, weight, preferred_element_type=f32).astype(bf16).astype(f32)
            at = pl.ds(t * WIDE, WIDE)
            agrad[b, at, :] = (hidden * slope[b, at, :]).astype(bf16)

    def norm_part(b, up):
        weight = wg[up].reshape(D, WIDE)
        for t in range(2):
            rows = agrad[b, pl.ds(t * WIDE, WIDE), :]
            rows = jnp.where(keep, rows, jnp.zeros_like(rows))
            product = lax.dot_general(rows, weight, (((1,), (1,)), ((), ())), preferred_element_type=f32)
            eight = pl.ds(t * 8, 8)
            part[eight] = product.reshape(8, 2, HALF, D)

            def one(p):
                sibs[b, p] = part[p, oc].astype(bf16)

            loop(t * 8, t * 8 + 8, one)
            remote(sibs.at[b, eight], sibr.at[b, eight], cs_s.at[b, t], cs_r.at[b, t], sibling).start()

    def rs_middle(b):
        for t in range(2):
            take(sibr.at[b, pl.ds(t * 8, 8)], cs_r.at[b, t])

            def one(k):
                p = t * 8 + lax.rem(gid + k, 8)

                @pl.when(p != gid)
                def _():
                    rss[b, p] = (part[p, c] + sibr[b, p].astype(f32)).astype(bf16)
                    remote(rss.at[b, p], rsr.at[b, gid], rs_s.at[b], rs_r.at[b], place(p)).start()

            loop(0, 8, one)

    def rs_finish(b, s):
        take(rsr.at[b, pl.ds(0, GROUP - 1)], rs_r.at[b])
        total = part[gid, c] + sibr[b, gid].astype(f32)

        def add(k, so_far):
            return so_far + rsr[b, other(k)].astype(f32)

        total = lax.fori_loop(1, GROUP, add, total)
        unit, inv_std = unit_rows(b)
        back = total * scl[s]
        back = inv_std * (
            back
            - jnp.mean(back, axis=-1, keepdims=True)
            - unit * jnp.mean(back * unit, axis=-1, keepdims=True)
        )
        return (full[2 * b, x, y, c].astype(f32) + back).astype(bf16)

    def weight_part(s, left_ref, right, lead):
        for low, size in ((0, 512), (512, 512), (1024, 640)):
            left = left_ref[lead + (slice(low, low + size),)].reshape(TOK, size)
            dwp[s, low : low + size, :] = lax.dot_general(
                left, right, (((0,), (0,)), ((), ())), preferred_element_type=f32
            )

    tokens = (slice(None), slice(None), slice(None))
    zag_take(3, 4)
    hidden_back(0, 3)
    zag(1, 1)
    zag(0, 1)
    ag_spread(1)
    zag_take(2, 4)
    norm_part(0, 2)
    weight_part(3, scaled.at[0], act[0], tokens)
    rs_middle(0)
    ag_send(3)
    zag(1, 2)
    zag(0, 2)
    zrs(3, 1)
    ag_forward(1)
    gelu_rows(1, 1, 0)
    ag_finish(1)
    weight_part(2, full.at[1], agrad[0], tokens + (slice(None),))
    zag(1, 3)
    zag(0, 3)
    zrs(2, 1)
    ag_spread(3)
    zrs(3, 2)
    full[2, x, y, c] = rs_finish(0, 2)
    ag_send(2)
    zag(1, 4)
    zag(0, 4)
    zrs(2, 2)
    ag_spread(2)
    zrs(3, 3)
    ag_forward(3)
    zrs(2, 3)
    ag_forward(2)
    ag_finish(3)
    ag_finish(2)
    scale_rows(1, 1)
    zag_take(1, 4)
    hidden_back(1, 1)
    weight_part(0, full.at[3], agrad[1], tokens + (slice(None),))
    zrs(0, 1)
    weight_part(1, scaled.at[1], act[1], tokens)
    zrs(1, 1)
    zag_take(0, 4)
    norm_part(1, 0)
    zrs(3, 4)
    zrs(2, 4)
    rs_middle(1)
    zrs(0, 2)
    zrs(1, 2)
    zrs_finish(3)
    zrs_finish(2)
    zrs(0, 3)
    zrs(1, 3)
    last = rs_finish(1, 0)

    @pl.when(y == 0)
    def _():
        g0f[0, c] = last

    @pl.when(y != 0)
    def _():
        g0s[...] = last
        remote(g0s, g0f.at[y, c], g0_s, g0_r, (0, dp, c)).start()

    zrs(0, 4)
    zrs(1, 4)
    zrs_finish(0)
    zrs_finish(1)

    @pl.when(y == 0)
    def _():
        take(g0f.at[pl.ds(1, NY - 1), 0], g0_r)
        half = g0f.at[:, c]
        remote(half, half, g1_s, g1_r, sibling).start()
        take(g0f.at[:, oc], g1_r)
        gout[...] = g0f[...].reshape(NY * ROWS, D)
        take(half, g1_s)

    @pl.when((y == 1) | (y == 2))
    def _():
        gout[...] = full[2, x].reshape(NY * ROWS, D)

    @pl.when(y == 3)
    def _():
        gout[...] = full[0, x].reshape(NY * ROWS, D)

    take(outr.at[pl.ds(0, GROUP - 1)], out_r)
    for p in range(GROUP):
        low = first_block(p) * LANE
        wout[:, low : low + WIDE] = outr[p, :OWN]

    take(wx.at[pl.ds(0, GROUP - 1)], wx_s)
    take(preb.at[pl.ds(0, GROUP - 1)], pre_s)
    take(scl.at[pl.ds(0, NY - 1)], sc_s)
    for b, s in ((0, 2), (1, 0)):

        @pl.when(y == s)
        def _():
            take(full.at[0, 0, pl.ds(0, NY - 1), 0], xi_s.at[b])

    for i in range(4):
        for k in range(1, NX):
            if i > 0:
                take(full.at[i, 0, 0, 0], ag_s.at[i, k])
                take(full.at[i, 0, :, 0], far_s.at[i, k])
        for k in range(NX):
            take(full.at[i, 0, :, 0], sib_s.at[i, k])
    for k in range(1, NX):

        @pl.when(c == 0)
        def _():
            take(full.at[0, 0, 0, 0], ag_s.at[0, k])
            take(full.at[0, 0, pl.ds(0, 3), 0], far_s.at[0, k])

        @pl.when(c == 1)
        def _():
            take(full.at[0, 0, :, 0], far_s.at[0, k])

    for b in range(2):
        for t in range(2):
            take(sibs.at[b, pl.ds(t * 8, 8)], cs_s.at[b, t])
        take(rss.at[b, pl.ds(0, GROUP - 1)], rs_s.at[b])
    for s in range(SECTIONS):
        for d in range(2):
            for k in range(1, 5):
                take(zag_block(s, 0, d, k), zag_s.at[s, d, k - 1])
                if k == 1:
                    take(zs.at[s, d, 0, :, pl.ds(d * LANE, LANE)], zrs_s.at[s, d, 0])
                else:
                    take(zs.at[s, d, k - 1], zrs_s.at[s, d, k - 1])
    take(outs.at[pl.ds(0, GROUP - 1)], out_s)

    @pl.when(y != 0)
    def _():
        take(g0s, g0_s)


def body(llm_grad, slot_row, counts, saved_in, saved_pre, weights, channel_scale):
    hidden = saved_pre.shape[3]
    pre = saved_pre.reshape(NY * ROWS, hidden)
    vmem = pl.BlockSpec(memory_space=pltpu.VMEM)
    anywhere = pl.BlockSpec(memory_space=pl.ANY)
    dma = pltpu.SemaphoreType.DMA
    scratch = [
        pltpu.VMEM((PAD, BLOCKS * LANE), bf16),
        pltpu.VMEM((GROUP, PAD, WIDE), bf16),
        pltpu.VMEM((SECTIONS, NZ, PACK, WIDE), bf16),
        pltpu.VMEM((GROUP, NY * ROWS, WIDE), bf16),
        pltpu.VMEM((4, NX, NY, 2, HALF, D), bf16),
        pltpu.VMEM((2, GROUP, 2, HALF, D), bf16),
        pltpu.VMEM((GROUP, 2, HALF, D), f32),
        pltpu.VMEM((2, GROUP, HALF, D), bf16),
        pltpu.VMEM((2, GROUP, HALF, D), bf16),
        pltpu.VMEM((2, GROUP, HALF, D), bf16),
        pltpu.VMEM((2, GROUP, HALF, D), bf16),
        pltpu.VMEM((2, TOK, WIDE), bf16),
        pltpu.VMEM((2, TOK, WIDE), f32),
        pltpu.VMEM((2, TOK, WIDE), bf16),
        pltpu.VMEM((SECTIONS, D, WIDE), f32),
        pltpu.VMEM((SECTIONS, 2, 4, PACK, WIDE), bf16),
        pltpu.VMEM((SECTIONS, 2, 4, PACK, WIDE), bf16),
        pltpu.VMEM((GROUP, PAD, WIDE), bf16),
        pltpu.VMEM((GROUP, PAD, WIDE), bf16),
        pltpu.VMEM((SECTIONS, 1, D), f32),
        pltpu.VMEM((2, HALF, D), bf16),
        pltpu.VMEM((NY, 2, HALF, D), bf16),
        pltpu.VMEM((HALF, D), bf16),
        dma((2,)), dma, dma, dma, dma, dma, dma, dma((2,)), dma((2,)),
        dma((4, 4)), dma((4, 4)), dma((4, 4)), dma((4, 4)), dma((4, 4)), dma((4, 4)), dma((2, 2)), dma((2, 2)), dma((2,)), dma((2,)),
        dma((4, 2, 4)), dma((4, 2, 4)), dma((4, 2, 4)), dma((4, 2, 4)), dma, dma, dma, dma, dma, dma,
    ]
    wout, gout = pl.pallas_call(
        kernel,
        out_shape=(
            jax.ShapeDtypeStruct((OWN, hidden), bf16),
            jax.ShapeDtypeStruct((NY * ROWS, D), bf16),
        ),
        in_specs=[vmem, vmem, pl.BlockSpec(memory_space=pltpu.SMEM), vmem, anywhere, vmem, vmem],
        out_specs=(vmem, vmem),
        scratch_shapes=scratch,
        compiler_params=pltpu.CompilerParams(
            collective_id=0, has_side_effects=True, vmem_limit_bytes=60 * 1024 * 1024
        ),
    )(llm_grad, slot_row[:, 0], counts, saved_in[0], pre, weights[0], channel_scale)
    return (wout[None], gout.reshape(1, NY, ROWS, D))


def solution(mesh):
    in_specs = (
        P(None, "dp", None),
        P(None, "dp", None),
        P("dp", None),
        P("pipe", None, "dp", None),
        P("pipe", None, "dp", "tensor"),
        P("pipe", "dp", "tensor"),
        P("pipe", None),
    )
    out_specs = (P("pipe", "dp", "tensor"), P("pipe", None, "dp", None))
    return jax.shard_map(body, mesh=mesh, in_specs=in_specs, out_specs=out_specs, check_vma=False)
```

```python
import functools

import jax
import jax.numpy as jnp
from jax import lax
from jax.experimental import pallas as pl
from jax.experimental.pallas import tpu as pltpu
from jax.sharding import PartitionSpec as P

norm_eps = 1e-06
root_half = 0.7071067811865476
inv_root_two_pi = 0.3989422804014327

MESH = pl.DeviceIdType.MESH
f32 = jnp.float32
bf16 = jnp.bfloat16

NX, NY, NZ = 4, 4, 8
GROUP = NX * NY
D = 1664
ROWS = 32
HALF = 16
TOK = 512
OWN = 52
PAD = 64
PACK = NX * OWN
LANE = 128
WIDE = 256
BLOCKS = 25
SECTIONS = 4


def first_block(piece):
    return (23 * piece) // 15


def gelu_value(p):
    return p * (0.5 * (1.0 + lax.erf(p * root_half)))


def gelu_slope(p):
    cdf = 0.5 * (1.0 + lax.erf(p * root_half))
    return cdf + p * (jnp.exp(-0.5 * p * p) * inv_root_two_pi)


def kernel(
    llm, slots, counts, xin, pre, w, scale,
    wout, gout,
    wpad, wx, wg, preb, full, scaled, part, sibs, sibr, rss, rsr, act, slope, agrad,
    dwp, zs, zr, outs, outr, scl, xi, g0f, g0s,
    local_sem, wx_s, wx_r, pre_s, pre_r, sc_s, sc_r, xi_s, xi_r,
    ag_s, ag_r, far_s, far_r, sib_s, sib_r, cs_s, cs_r, rs_s, rs_r,
    zag_s, zag_r, zrs_s, zrs_r, out_s, out_r, g0_s, g0_r, g1_s, g1_r,
):
    y = lax.axis_index("pipe")
    dp = lax.axis_index("dp")
    c = lax.axis_index("tensor")
    z = lax.div(dp, NX)
    x = lax.rem(dp, NX)
    gid = x * NY + y
    oc = 1 - c
    sibling = (y, dp, oc)
    up_z = (y, lax.rem(z + 1, NZ) * NX + x, c)
    down_z = (y, lax.rem(z + NZ - 1, NZ) * NX + x, c)

    def place(piece):
        return (lax.rem(piece, NY), z * NX + lax.div(piece, NY), c)

    def other(k):
        return lax.rem(gid + k, GROUP)

    def loop(low, high, body):
        def step(k, carry):
            body(k)
            return carry

        lax.fori_loop(low, high, step, 0)

    def remote(src, dst, send, recv, where):
        return pltpu.make_async_remote_copy(
            src_ref=src, dst_ref=dst, send_sem=send, recv_sem=recv, device_id=where, device_id_type=MESH
        )

    def take(ref, sem):
        pltpu.make_async_copy(ref, ref, sem).wait()

    def is_narrow(piece):
        return (lax.rem(piece, 2) == 1) & (piece < 14)

    slim = is_narrow(gid)
    broad = jnp.logical_not(slim)
    upper = pl.ds(LANE, LANE)

    def put(src, dst, piece, send, recv):
        low = lax.div(23 * piece, 15) * LANE

        @pl.when(is_narrow(piece))
        def _():
            part_src = src.at[:, pl.ds(pl.multiple_of(low + LANE, LANE), LANE)]
            remote(part_src, dst.at[:, upper], send.at[1], recv, place(piece)).start()

        @pl.when(jnp.logical_not(is_narrow(piece)))
        def _():
            part_src = src.at[:, pl.ds(pl.multiple_of(low, LANE), WIDE)]
            remote(part_src, dst, send.at[0], recv, place(piece)).start()

    def keep_own(src, dst, sem):
        low = lax.div(23 * gid, 15) * LANE

        @pl.when(slim)
        def _():
            part_src = src.at[:, pl.ds(pl.multiple_of(low + LANE, LANE), LANE)]
            pltpu.make_async_copy(part_src, dst.at[:, upper], sem).start()

        @pl.when(broad)
        def _():
            part_src = src.at[:, pl.ds(pl.multiple_of(low, LANE), WIDE)]
            pltpu.make_async_copy(part_src, dst, sem).start()

    def take_pieces(ref, low, size, sem):
        @pl.when(slim)
        def _():
            take(ref.at[pl.ds(low, size), :, upper], sem)

        @pl.when(broad)
        def _():
            take(ref.at[pl.ds(low, size)], sem)

    def take_mixed(ref, sem):
        @pl.when(slim)
        def _():
            take(ref.at[pl.ds(0, 9)], sem.at[0])
            take(ref.at[pl.ds(0, 6), :, upper], sem.at[1])

        @pl.when(broad)
        def _():
            take(ref.at[pl.ds(0, 8)], sem.at[0])
            take(ref.at[pl.ds(0, 7), :, upper], sem.at[1])

    barrier = pltpu.get_barrier_semaphore()

    def greet(k):
        pl.semaphore_signal(barrier, inc=1, device_id=place(other(k)), device_id_type=MESH)

    loop(1, GROUP, greet)
    for where in (sibling, up_z, down_z):
        pl.semaphore_signal(barrier, inc=1, device_id=where, device_id_type=MESH)
    keep_own(pre, preb.at[y * NX + x], local_sem.at[1])

    @pl.when(slim)
    def _():
        wx[:, :, :LANE] = jnp.zeros((GROUP, PAD, LANE), bf16)
        preb[:, :, :LANE] = jnp.zeros((GROUP, NY * ROWS, LANE), bf16)

    wpad[:OWN, :] = w[...]
    wpad[OWN:, :] = jnp.zeros((PAD - OWN, BLOCKS * LANE), bf16)
    keep_own(wpad, wx.at[y * NX + x], local_sem.at[0])
    scl[y] = scale[...]
    half_rows = pl.ds(pl.multiple_of(c * HALF, HALF), HALF)
    row_ids = lax.broadcasted_iota(jnp.int32, (HALF, ROWS), 0) + c * HALF
    slot_ids = lax.broadcasted_iota(jnp.int32, (HALF, ROWS), 1)
    for m in range(NY):
        hit = (slots[m : m + 1, :] == row_ids) & (slot_ids < counts[0, m])
        onehot = jnp.where(hit, 1.0, 0.0).astype(bf16)
        full[0, x, m, c] = jnp.dot(onehot, llm[m], preferred_element_type=f32).astype(bf16)
    for b, s in ((0, 2), (1, 0)):

        @pl.when(y == s)
        def _():
            xi[b] = xin[y, half_rows, :]

    pl.semaphore_wait(barrier, GROUP + 2)

    def send_w(k):
        put(wpad, wx.at[y * NX + x], other(k), wx_s, wx_r)

    loop(1, GROUP, send_w)

    def send_scale(k):
        py = lax.rem(y + k, NY)
        remote(scale, scl.at[y], sc_s, sc_r, (py, dp, c)).start()

    loop(1, NY, send_scale)

    def near(k):
        return lax.rem(x + k * (1 - c), NX), lax.rem(y + k * c, NY)

    def far(k):
        return lax.rem(x + k * c, NX), lax.rem(y + k * (1 - c), NY)

    def spread(i, q):
        px, py = near(q)
        piece = full.at[i, px, py, c]

        def send(k):
            fx, fy = far(k)
            remote(piece, piece, far_s.at[i, k], far_r.at[i, NX - k], (fy, z * NX + fx, c)).start()

        loop(1, NX, send)

    def ag_near(i):
        piece = full.at[i, x, y, c]

        def send(k):
            px, py = near(k)
            remote(piece, piece, ag_s.at[i, k], ag_r.at[i, NX - k], (py, z * NX + px, c)).start()

        loop(1, NX, send)

    def ag_send(i):
        ag_near(i)
        spread(i, 0)

    def ag_far(i):
        spread(i, 0)
        ag_spread(i)

    def ag_spread(i):
        for q in (1, 3, 2):
            take(full.at[i, 0, 0, 0], ag_r.at[i, q])
            spread(i, q)
        give(i, 0)

    def give(i, k):
        fx, fy = far(k)

        @pl.when(c == 0)
        def _():
            four = full.at[i, :, fy, 0]
            remote(four, four, sib_s.at[i, k], sib_r.at[i, k], sibling).start()

        @pl.when(c == 1)
        def _():
            four = full.at[i, fx, :, 1]
            remote(four, four, sib_s.at[i, k], sib_r.at[i, k], sibling).start()

    def ag_forward(i):
        for k in (1, 3, 2):
            take(full.at[i, 0, :, 0], far_r.at[i, k])
            give(i, k)

    def ag_finish(i):
        for k in range(NX):
            take(full.at[i, 0, :, 0], sib_r.at[i, k])

    def top_send():
        @pl.when(c == 0)
        def _():
            piece = full.at[0, x, y, 0]

            def send(k):
                px, py = near(k)
                remote(piece, piece, ag_s.at[0, k], ag_r.at[0, NX - k], (py, z * NX + px, c)).start()

            loop(1, NX, send)

        @pl.when(c == 1)
        def _():
            four = full.at[0, x, :, 1]

            def send(k):
                fx, fy = far(k)
                remote(four, four, far_s.at[0, k], far_r.at[0, NX - k], (fy, z * NX + fx, c)).start()

            loop(1, NX, send)
            give(0, 0)

    def top_spread():
        @pl.when(c == 0)
        def _():
            for q in (1, 3, 2):
                take(full.at[0, 0, 0, 0], ag_r.at[0, q])
                spread(0, q)
            give(0, 0)

    def top_forward():
        for k in (1, 3, 2):

            @pl.when(c == 0)
            def _():
                take(full.at[0, 0, pl.ds(0, 3), 0], far_r.at[0, k])

            @pl.when(c == 1)
            def _():
                take(full.at[0, 0, :, 0], far_r.at[0, k])

            give(0, k)

    def send_pre(k):
        put(pre, preb.at[y * NX + x], other(k), pre_s, pre_r)

    def rows_send():
        for b, s in ((0, 2), (1, 0)):

            @pl.when(y == s)
            def _():
                def send(k):
                    py = lax.rem(y + k, NY)
                    remote(xin.at[py, half_rows, :], xi.at[b], xi_s.at[b], xi_r.at[b], (py, dp, c)).start()

                loop(1, NY, send)

    to_row = lax.broadcasted_iota(jnp.int32, (PACK, NX * PAD), 0)
    from_row = lax.broadcasted_iota(jnp.int32, (PACK, NX * PAD), 1)
    from_block = lax.shift_right_logical(from_row, 6)
    inside = from_row - from_block * PAD
    picks = (inside < OWN) & (from_block * OWN + inside == to_row)
    pick = jnp.where(picks, 1.0, 0.0).astype(bf16)

    def pack(s):
        blocks = wx[s * NX : (s + 1) * NX].reshape(NX * PAD, WIDE)
        wg[s, z] = jnp.dot(pick, blocks, preferred_element_type=f32).astype(bf16)

    def zag_block(s, chunk, d, k):
        if k == 4:
            return wg.at[s, chunk, :, pl.ds(d * LANE, LANE)]
        return wg.at[s, chunk]

    def zag_take(s, k):
        for d, chunk in ((0, lax.rem(z - k + NZ, NZ)), (1, lax.rem(z + k, NZ))):
            take(zag_block(s, chunk, d, k), zag_r.at[s, d, k - 1])

    def zag(s, k):
        if k > 1:
            zag_take(s, k - 1)
        for d, chunk, where in (
            (0, lax.rem(z - k + 1 + NZ, NZ), up_z),
            (1, lax.rem(z + k - 1, NZ), down_z),
        ):
            block = zag_block(s, chunk, d, k)
            remote(block, block, zag_s.at[s, d, k - 1], zag_r.at[s, d, k - 1], where).start()

    def zrs(s, k):
        ways = ((0, lax.rem(z + 5 - k + NZ, NZ), up_z), (1, lax.rem(z - 5 + k + NZ, NZ), down_z))
        for d, chunk, where in ways:
            rows = pl.ds(pl.multiple_of(chunk * PACK, HALF), PACK)
            side = pl.ds(d * LANE, LANE)
            if k == 1:
                zs[s, d, 0, :, side] = dwp[s, rows, side].astype(bf16)
                src, dst = zs.at[s, d, 0, :, side], zr.at[s, d, 0, :, side]
            else:
                if k == 2:
                    take(zr.at[s, d, 0, :, side], zrs_r.at[s, d, 0])
                    there = pl.ds((1 - d) * LANE, LANE)
                    zs[s, d, 1, :, side] = (dwp[s, rows, side] + zr[s, d, 0, :, side].astype(f32)).astype(bf16)
                    zs[s, d, 1, :, there] = dwp[s, rows, there].astype(bf16)
                else:
                    take(zr.at[s, d, k - 2], zrs_r.at[s, d, k - 2])
                    zs[s, d, k - 1] = (dwp[s, rows, :] + zr[s, d, k - 2].astype(f32)).astype(bf16)
                src, dst = zs.at[s, d, k - 1], zr.at[s, d, k - 1]
            remote(src, dst, zrs_s.at[s, d, k - 1], zrs_r.at[s, d, k - 1], where).start()

    def zrs_finish(s):
        for d in range(2):
            take(zr.at[s, d, 3], zrs_r.at[s, d, 3])
        rows = pl.ds(pl.multiple_of(z * PACK, HALF), PACK)
        total = dwp[s, rows, :] + zr[s, 0, 3].astype(f32) + zr[s, 1, 3].astype(f32)
        spread = lax.dot_general(pick, total.astype(bf16), (((0,), (0,)), ((), ())), preferred_element_type=f32)
        outs[s * NX : (s + 1) * NX] = spread.astype(bf16).reshape(NX, PAD, WIDE)

        def send(px):
            mine = (y == s) & (px == x)

            @pl.when(mine)
            def _():
                outr[gid] = outs[s * NX + px]

            where = (s, z * NX + px, c)

            @pl.when(jnp.logical_not(mine) & slim)
            def _():
                src, dst = outs.at[s * NX + px, :, upper], outr.at[gid, :, upper]
                remote(src, dst, out_s, out_r.at[1], where).start()

            @pl.when(jnp.logical_not(mine) & broad)
            def _():
                remote(outs.at[s * NX + px], outr.at[gid], out_s, out_r.at[0], where).start()

        loop(0, NX, send)

    def unit_rows(b):
        values = xi[b].astype(f32)
        center = values - jnp.mean(values, axis=-1, keepdims=True)
        inv_std = lax.rsqrt(jnp.mean(center * center, axis=-1, keepdims=True) + norm_eps)
        return center * inv_std, inv_std

    def norm_rows(b, s):
        @pl.when(y != s)
        def _():
            take(xi.at[b], xi_r.at[b])

        unit, inv_std = unit_rows(b)
        full[1 + 2 * b, x, y, c] = (unit * scl[s]).astype(bf16)

    def scale_rows(i, s):
        def one(p):
            rows = full[2 * i, lax.div(p, NY), lax.rem(p, NY)].astype(f32) * scl[s]
            scaled[i, p] = rows.astype(bf16)

        loop(0, GROUP, one)

    def value_rows(b, s):
        def one(p):
            rows = pl.ds(pl.multiple_of(lax.rem(p, NY) * ROWS, ROWS), ROWS)
            at = pl.ds(pl.multiple_of(p * ROWS, ROWS), ROWS)
            act[b, at, :] = gelu_value(preb[s * NX + lax.div(p, NY), rows, :].astype(f32)).astype(bf16)

        loop(0, GROUP, one)

    def slope_rows(b, s):
        def one(p):
            rows = pl.ds(pl.multiple_of(lax.rem(p, NY) * ROWS, ROWS), ROWS)
            at = pl.ds(pl.multiple_of(p * ROWS, ROWS), ROWS)
            slope[b, at, :] = gelu_slope(preb[s * NX + lax.div(p, NY), rows, :].astype(f32))

        loop(0, GROUP, one)

    def hidden_back(b, down):
        weight = wg[down].reshape(D, WIDE)
        for t in range(2):
            left = scaled[b, t * 8 : t * 8 + 8].reshape(WIDE, D)
            hidden = jnp.dot(left, weight, preferred_element_type=f32).astype(bf16).astype(f32)
            at = pl.ds(t * WIDE, WIDE)
            agrad[b, at, :] = (hidden * slope[b, at, :]).astype(bf16)

    def norm_part(b, up):
        weight = wg[up].reshape(D, WIDE)
        for t in range(2):
            rows = agrad[b, pl.ds(t * WIDE, WIDE), :]
            product = lax.dot_general(rows, weight, (((1,), (1,)), ((), ())), preferred_element_type=f32)
            eight = pl.ds(t * 8, 8)
            part[eight] = product.reshape(8, 2, HALF, D)

            def one(p):
                sibs[b, p] = part[p, oc].astype(bf16)

            loop(t * 8, t * 8 + 8, one)
            remote(sibs.at[b, eight], sibr.at[b, eight], cs_s.at[b, t], cs_r.at[b, t], sibling).start()

    def rs_middle(b):
        for t in range(2):
            take(sibr.at[b, pl.ds(t * 8, 8)], cs_r.at[b, t])

            def one(k):
                p = t * 8 + lax.rem(gid + k, 8)

                @pl.when(p != gid)
                def _():
                    rss[b, p] = (part[p, c] + sibr[b, p].astype(f32)).astype(bf16)
                    remote(rss.at[b, p], rsr.at[b, gid], rs_s.at[b], rs_r.at[b], place(p)).start()

            loop(0, 8, one)

    def rs_finish(b, s):
        take(rsr.at[b, pl.ds(0, GROUP - 1)], rs_r.at[b])
        total = part[gid, c] + sibr[b, gid].astype(f32)

        def add(k, so_far):
            return so_far + rsr[b, other(k)].astype(f32)

        total = lax.fori_loop(1, GROUP, add, total)
        unit, inv_std = unit_rows(b)
        back = total * scl[s]
        back = inv_std * (
            back
            - jnp.mean(back, axis=-1, keepdims=True)
            - unit * jnp.mean(back * unit, axis=-1, keepdims=True)
        )
        return (full[2 * b, x, y, c].astype(f32) + back).astype(bf16)

    def weight_part(s, left_ref, right, lead):
        for low, size in ((0, 512), (512, 512), (1024, 640)):
            left = left_ref[lead + (slice(low, low + size),)].reshape(TOK, size)
            dwp[s, low : low + size, :] = lax.dot_general(
                left, right, (((0,), (0,)), ((), ())), preferred_element_type=f32
            )

    def last_rows():
        last = rs_finish(1, 0)

        @pl.when(y == 0)
        def _():
            g0f[0, c] = last

        @pl.when(y != 0)
        def _():
            g0s[...] = last
            remote(g0s, g0f.at[y, c], g0_s, g0_r, (0, dp, c)).start()

    def rows_out():
        @pl.when(y == 0)
        def _():
            take(g0f.at[pl.ds(1, NY - 1), 0], g0_r)
            half = g0f.at[:, c]
            remote(half, half, g1_s, g1_r, sibling).start()
            take(g0f.at[:, oc], g1_r)
            gout[...] = g0f[...].reshape(NY * ROWS, D)
            take(half, g1_s)

        @pl.when((y == 1) | (y == 2))
        def _():
            gout[...] = full[2, x].reshape(NY * ROWS, D)

        @pl.when(y == 3)
        def _():
            gout[...] = full[0, x].reshape(NY * ROWS, D)

    tokens = (slice(None), slice(None), slice(None))
    every = tokens + (slice(None),)

    def first_drain():
        take_mixed(wx, wx_s)
        take_mixed(preb, pre_s)
        take(scl.at[pl.ds(0, NY - 1)], sc_s)
        for b, s in ((0, 2), (1, 0)):

            @pl.when(y == s)
            def _():
                take(full.at[0, 0, pl.ds(0, NY - 1), 0], xi_s.at[b])

        for i in range(4):
            for k in range(1, NX):
                if i > 0:
                    take(full.at[i, 0, 0, 0], ag_s.at[i, k])
                    take(full.at[i, 0, :, 0], far_s.at[i, k])
            for k in range(NX):
                take(full.at[i, 0, :, 0], sib_s.at[i, k])
        for k in range(1, NX):

            @pl.when(c == 0)
            def _():
                take(full.at[0, 0, 0, 0], ag_s.at[0, k])
                take(full.at[0, 0, pl.ds(0, 3), 0], far_s.at[0, k])

            @pl.when(c == 1)
            def _():
                take(full.at[0, 0, :, 0], far_s.at[0, k])

        for s in range(SECTIONS):
            for d in range(2):
                for k in range(1, 5):
                    take(zag_block(s, 0, d, k), zag_s.at[s, d, k - 1])

    def rs_drain(b):
        for t in range(2):
            take(sibs.at[b, pl.ds(t * 8, 8)], cs_s.at[b, t])
        take(rss.at[b, pl.ds(0, GROUP - 1)], rs_s.at[b])

    def zrs_drain(s):
        for d in range(2):
            take(zs.at[s, d, 0, :, pl.ds(d * LANE, LANE)], zrs_s.at[s, d, 0])
            for k in range(2, 5):
                take(zs.at[s, d, k - 1], zrs_s.at[s, d, k - 1])

    def weights_in():
        take_pieces(wx, 0, GROUP - 1, wx_r)
        take_pieces(wx, 0, 1, local_sem.at[0])

    def pre_in():
        take_pieces(preb, 0, GROUP - 1, pre_r)
        take_pieces(preb, 0, 1, local_sem.at[1])

    top_send()
    rows_send()
    weights_in()
    pack(3)
    zag(3, 1)
    pack(2)
    zag(2, 1)
    top_spread()
    loop(1, GROUP, send_pre)
    pack(1)
    pack(0)
    take(scl.at[pl.ds(0, NY - 1)], sc_r)
    norm_rows(0, 2)
    norm_rows(1, 0)
    ag_near(1)
    ag_near(3)
    zag(3, 2)
    zag(2, 2)
    zag(3, 3)
    zag(2, 3)
    zag(1, 1)
    top_forward()
    ag_finish(0)
    scale_rows(0, 3)
    zag(3, 4)
    zag(2, 4)
    zag(0, 1)
    pre_in()
    ag_far(1)
    slope_rows(0, 2)
    zag_take(3, 4)
    hidden_back(0, 3)
    zag_take(2, 4)
    norm_part(0, 2)
    zag(1, 2)
    value_rows(0, 3)
    weight_part(3, scaled.at[0], act[0], tokens)
    rs_middle(0)
    zrs(3, 1)
    zag(0, 2)
    value_rows(1, 1)
    slope_rows(1, 0)
    ag_forward(1)
    zag(1, 3)
    zag(0, 3)
    ag_finish(1)
    weight_part(2, full.at[1], agrad[0], every)
    zrs(2, 1)
    zrs(3, 2)
    zag(1, 4)
    full[2, x, y, c] = rs_finish(0, 2)
    ag_send(2)
    ag_far(3)
    zag(0, 4)
    ag_spread(2)
    zrs(3, 3)
    zrs(2, 2)
    ag_forward(3)
    ag_forward(2)
    ag_finish(2)
    scale_rows(1, 1)
    weight_part(1, scaled.at[1], act[1], tokens)
    zrs(1, 1)
    zag_take(1, 4)
    hidden_back(1, 1)
    zag_take(0, 4)
    norm_part(1, 0)
    ag_finish(3)
    weight_part(0, full.at[3], agrad[1], every)
    zrs(0, 1)
    zrs(3, 4)
    zrs(2, 3)
    rs_middle(1)
    zrs(1, 2)
    zrs(0, 2)
    zrs(2, 4)
    zrs_finish(3)
    first_drain()
    zrs(1, 3)
    zrs(0, 3)
    zrs_finish(2)
    rs_drain(0)
    last_rows()
    zrs(1, 4)
    zrs(0, 4)
    zrs_drain(3)
    zrs_drain(2)
    rs_drain(1)
    zrs_finish(1)
    zrs_finish(0)
    rows_out()
    zrs_drain(1)
    zrs_drain(0)
    take_mixed(outr, out_r)
    for p in range(GROUP):
        skip = LANE if p % 2 == 1 and p < 14 else 0
        low = first_block(p) * LANE
        wout[:, low + skip : low + WIDE] = outr[p, :OWN, skip:]
    take_pieces(outs, 0, GROUP - 1, out_s)

    @pl.when(y != 0)
    def _():
        take(g0s, g0_s)


def body(llm_grad, slot_row, counts, saved_in, saved_pre, weights, channel_scale):
    hidden = saved_pre.shape[3]
    pre = saved_pre.reshape(NY * ROWS, hidden)
    vmem = pl.BlockSpec(memory_space=pltpu.VMEM)
    anywhere = pl.BlockSpec(memory_space=pl.ANY)
    dma = pltpu.SemaphoreType.DMA
    scratch = [
        pltpu.VMEM((PAD, BLOCKS * LANE), bf16),
        pltpu.VMEM((GROUP, PAD, WIDE), bf16),
        pltpu.VMEM((SECTIONS, NZ, PACK, WIDE), bf16),
        pltpu.VMEM((GROUP, NY * ROWS, WIDE), bf16),
        pltpu.VMEM((4, NX, NY, 2, HALF, D), bf16),
        pltpu.VMEM((2, GROUP, 2, HALF, D), bf16),
        pltpu.VMEM((GROUP, 2, HALF, D), f32),
        pltpu.VMEM((2, GROUP, HALF, D), bf16),
        pltpu.VMEM((2, GROUP, HALF, D), bf16),
        pltpu.VMEM((2, GROUP, HALF, D), bf16),
        pltpu.VMEM((2, GROUP, HALF, D), bf16),
        pltpu.VMEM((2, TOK, WIDE), bf16),
        pltpu.VMEM((2, TOK, WIDE), f32),
        pltpu.VMEM((2, TOK, WIDE), bf16),
        pltpu.VMEM((SECTIONS, D, WIDE), f32),
        pltpu.VMEM((SECTIONS, 2, 4, PACK, WIDE), bf16),
        pltpu.VMEM((SECTIONS, 2, 4, PACK, WIDE), bf16),
        pltpu.VMEM((GROUP, PAD, WIDE), bf16),
        pltpu.VMEM((GROUP, PAD, WIDE), bf16),
        pltpu.VMEM((SECTIONS, 1, D), f32),
        pltpu.VMEM((2, HALF, D), bf16),
        pltpu.VMEM((NY, 2, HALF, D), bf16),
        pltpu.VMEM((HALF, D), bf16),
        dma((2,)), dma((2,)), dma, dma((2,)), dma, dma, dma, dma((2,)), dma((2,)),
        dma((4, 4)), dma((4, 4)), dma((4, 4)), dma((4, 4)), dma((4, 4)), dma((4, 4)), dma((2, 2)), dma((2, 2)), dma((2,)), dma((2,)),
        dma((4, 2, 4)), dma((4, 2, 4)), dma((4, 2, 4)), dma((4, 2, 4)), dma, dma((2,)), dma, dma, dma, dma,
    ]
    wout, gout = pl.pallas_call(
        kernel,
        out_shape=(
            jax.ShapeDtypeStruct((OWN, hidden), bf16),
            jax.ShapeDtypeStruct((NY * ROWS, D), bf16),
        ),
        in_specs=[vmem, vmem, pl.BlockSpec(memory_space=pltpu.SMEM), vmem, anywhere, vmem, vmem],
        out_specs=(vmem, vmem),
        scratch_shapes=scratch,
        compiler_params=pltpu.CompilerParams(
            collective_id=0, has_side_effects=True, vmem_limit_bytes=60 * 1024 * 1024
        ),
    )(llm_grad, slot_row[:, 0], counts, saved_in[0], pre, weights[0], channel_scale)
    return (wout[None], gout.reshape(1, NY, ROWS, D))


def solution(mesh):
    in_specs = (
        P(None, "dp", None),
        P(None, "dp", None),
        P("dp", None),
        P("pipe", None, "dp", None),
        P("pipe", None, "dp", "tensor"),
        P("pipe", "dp", "tensor"),
        P("pipe", None),
    )
    out_specs = (P("pipe", "dp", "tensor"), P("pipe", None, "dp", None))
    return jax.shard_map(body, mesh=mesh, in_specs=in_specs, out_specs=out_specs, check_vma=False)
```

```python
import functools

import jax
import jax.numpy as jnp
from jax import lax
from jax.experimental import pallas as pl
from jax.experimental.pallas import tpu as pltpu
from jax.sharding import PartitionSpec as P

norm_eps = 1e-06
root_half = 0.7071067811865476
inv_root_two_pi = 0.3989422804014327

MESH = pl.DeviceIdType.MESH
f32 = jnp.float32
bf16 = jnp.bfloat16

NX, NY, NZ = 4, 4, 8
GROUP = NX * NY
D = 1664
ROWS = 32
HALF = 16
TOK = 512
OWN = 52
PAD = 64
PACK = NX * OWN
LANE = 128
WIDE = 256
BLOCKS = 25
SECTIONS = 4


def first_block(piece):
    return (23 * piece) // 15


def gelu_value(p):
    return p * (0.5 * (1.0 + lax.erf(p * root_half)))


def gelu_slope(p):
    cdf = 0.5 * (1.0 + lax.erf(p * root_half))
    return cdf + p * (jnp.exp(-0.5 * p * p) * inv_root_two_pi)


def kernel(
    llm, slots, counts, xin, pre, w, scale,
    wout, gout,
    wpad, wx, wg, preb, full, scaled, part, wsib, psib, asib, rss, rsr, act, slope, agrad,
    dwp, zs, zr, outs, outr, scl, xi, g0f, g0s,
    local_sem, wx_s, wx_r, pre_s, pre_r, sc_s, sc_r, xi_s, xi_r,
    ag_s, ag_r, far_s, far_r, sib_s, sib_r, ws_s, ws_r, ps_s, ps_r, as_s, as_r, rs_s, rs_r,
    zag_s, zag_r, zrs_s, zrs_r, out_s, out_r, g0_s, g0_r,
):
    y = lax.axis_index("pipe")
    dp = lax.axis_index("dp")
    c = lax.axis_index("tensor")
    z = lax.div(dp, NX)
    x = lax.rem(dp, NX)
    gid = x * NY + y
    oc = 1 - c
    sibling = (y, dp, oc)
    up_z = (y, lax.rem(z + 1, NZ) * NX + x, c)
    down_z = (y, lax.rem(z + NZ - 1, NZ) * NX + x, c)

    def place(piece):
        return (lax.rem(piece, NY), z * NX + lax.div(piece, NY), c)

    def other(k):
        return lax.rem(gid + k, GROUP)

    def loop(low, high, body):
        def step(k, carry):
            body(k)
            return carry

        lax.fori_loop(low, high, step, 0)

    def remote(src, dst, send, recv, where):
        return pltpu.make_async_remote_copy(
            src_ref=src, dst_ref=dst, send_sem=send, recv_sem=recv, device_id=where, device_id_type=MESH
        )

    def take(ref, sem):
        pltpu.make_async_copy(ref, ref, sem).wait()

    def is_narrow(piece):
        return (lax.rem(piece, 2) == 1) & (piece < 14)

    slim = is_narrow(gid)
    broad = jnp.logical_not(slim)
    upper = pl.ds(LANE, LANE)
    one_dim = (slice(None),)
    tokens = (slice(None), slice(None), slice(None))
    every = tokens + one_dim

    def put(src, dst, piece, send, recv, lead):
        low = lax.div(23 * piece, 15) * LANE

        @pl.when(is_narrow(piece))
        def _():
            part_src = src.at[lead + (pl.ds(pl.multiple_of(low + LANE, LANE), LANE),)]
            remote(part_src, dst.at[lead + (upper,)], send.at[1], recv, place(piece)).start()

        @pl.when(jnp.logical_not(is_narrow(piece)))
        def _():
            part_src = src.at[lead + (pl.ds(pl.multiple_of(low, LANE), WIDE),)]
            remote(part_src, dst, send.at[0], recv, place(piece)).start()

    def keep_own(src, dst, sem, lead):
        low = lax.div(23 * gid, 15) * LANE

        @pl.when(slim)
        def _():
            part_src = src.at[lead + (pl.ds(pl.multiple_of(low + LANE, LANE), LANE),)]
            pltpu.make_async_copy(part_src, dst.at[lead + (upper,)], sem).start()

        @pl.when(broad)
        def _():
            part_src = src.at[lead + (pl.ds(pl.multiple_of(low, LANE), WIDE),)]
            pltpu.make_async_copy(part_src, dst, sem).start()

    def take_pieces(ref, low, size, sem, lead):
        @pl.when(slim)
        def _():
            take(ref.at[(pl.ds(low, size),) + lead + (upper,)], sem)

        @pl.when(broad)
        def _():
            take(ref.at[pl.ds(low, size)], sem)

    def take_mixed(ref, sem, lead):
        @pl.when(slim)
        def _():
            take(ref.at[pl.ds(0, 9)], sem.at[0])
            take(ref.at[(pl.ds(0, 6),) + lead + (upper,)], sem.at[1])

        @pl.when(broad)
        def _():
            take(ref.at[pl.ds(0, 8)], sem.at[0])
            take(ref.at[(pl.ds(0, 7),) + lead + (upper,)], sem.at[1])

    barrier = pltpu.get_barrier_semaphore()

    def greet(k):
        pl.semaphore_signal(barrier, inc=1, device_id=place(other(k)), device_id_type=MESH)

    loop(1, GROUP, greet)
    for where in (sibling, up_z, down_z):
        pl.semaphore_signal(barrier, inc=1, device_id=where, device_id_type=MESH)
    def greet_across(k):
        where = (lax.rem(y + k, NY), dp, oc)
        pl.semaphore_signal(barrier, inc=1, device_id=where, device_id_type=MESH)

    loop(1, NY, greet_across)
    keep_own(pre, preb.at[y * NX + x], local_sem.at[1], tokens)

    @pl.when(slim)
    def _():
        wx[:, :, :LANE] = jnp.zeros((GROUP, PAD, LANE), bf16)
        preb[:, :, :, :, :LANE] = jnp.zeros((GROUP, NY, 2, HALF, LANE), bf16)

    wpad[:OWN, :] = w[...]
    wpad[OWN:, :] = jnp.zeros((PAD - OWN, BLOCKS * LANE), bf16)
    keep_own(wpad, wx.at[y * NX + x], local_sem.at[0], one_dim)
    scl[y] = scale[...]
    half_rows = pl.ds(pl.multiple_of(c * HALF, HALF), HALF)
    row_ids = lax.broadcasted_iota(jnp.int32, (HALF, ROWS), 0) + c * HALF
    slot_ids = lax.broadcasted_iota(jnp.int32, (HALF, ROWS), 1)
    for m in range(NY):
        hit = (slots[m : m + 1, :] == row_ids) & (slot_ids < counts[0, m])
        onehot = jnp.where(hit, 1.0, 0.0).astype(bf16)
        full[0, x, m, c] = jnp.dot(onehot, llm[m], preferred_element_type=f32).astype(bf16)
    for b, s in ((0, 2), (1, 0)):

        @pl.when(y == s)
        def _():
            xi[b] = xin[y, half_rows, :]

    pl.semaphore_wait(barrier, GROUP + NY + 1)

    def send_w(k):
        put(wpad, wx.at[y * NX + x], other(k), wx_s, wx_r, one_dim)

    loop(1, GROUP, send_w)

    def send_scale(k):
        py = lax.rem(y + k, NY)
        remote(scale, scl.at[y], sc_s, sc_r, (py, dp, c)).start()

    loop(1, NY, send_scale)

    def near(k):
        return lax.rem(x + k * (1 - c), NX), lax.rem(y + k * c, NY)

    def far(k):
        return lax.rem(x + k * c, NX), lax.rem(y + k * (1 - c), NY)

    def spread(i, q):
        px, py = near(q)
        piece = full.at[i, px, py, c]

        def send(k):
            fx, fy = far(k)
            remote(piece, piece, far_s.at[i, k], far_r.at[i, NX - k], (fy, z * NX + fx, c)).start()

        loop(1, NX, send)

    def ag_near(i):
        piece = full.at[i, x, y, c]

        def send(k):
            px, py = near(k)
            remote(piece, piece, ag_s.at[i, k], ag_r.at[i, NX - k], (py, z * NX + px, c)).start()

        loop(1, NX, send)

    def ag_send(i):
        ag_near(i)
        spread(i, 0)

    def ag_far(i):
        spread(i, 0)
        ag_spread(i)

    def ag_spread(i):
        for q in (1, 3, 2):
            take(full.at[i, 0, 0, 0], ag_r.at[i, q])
            spread(i, q)
        give(i, 0)

    def give(i, k):
        fx, fy = far(k)

        @pl.when(c == 0)
        def _():
            four = full.at[i, :, fy, 0]
            remote(four, four, sib_s.at[i, k], sib_r.at[i, k], sibling).start()

        @pl.when(c == 1)
        def _():
            four = full.at[i, fx, :, 1]
            remote(four, four, sib_s.at[i, k], sib_r.at[i, k], sibling).start()

    def ag_forward(i):
        for k in (1, 3, 2):
            take(full.at[i, 0, :, 0], far_r.at[i, k])
            give(i, k)

    def ag_finish(i):
        for k in range(NX):
            take(full.at[i, 0, :, 0], sib_r.at[i, k])

    def top_send():
        @pl.when(c == 0)
        def _():
            piece = full.at[0, x, y, 0]

            def send(k):
                px, py = near(k)
                remote(piece, piece, ag_s.at[0, k], ag_r.at[0, NX - k], (py, z * NX + px, c)).start()

            loop(1, NX, send)

        @pl.when(c == 1)
        def _():
            four = full.at[0, x, :, 1]

            def send(k):
                fx, fy = far(k)
                remote(four, four, far_s.at[0, k], far_r.at[0, NX - k], (fy, z * NX + fx, c)).start()

            loop(1, NX, send)
            give(0, 0)

    def top_spread():
        @pl.when(c == 0)
        def _():
            for q in (1, 3, 2):
                take(full.at[0, 0, 0, 0], ag_r.at[0, q])
                spread(0, q)
            give(0, 0)

    def top_forward():
        for k in (1, 3, 2):

            @pl.when(c == 0)
            def _():
                take(full.at[0, 0, pl.ds(0, 3), 0], far_r.at[0, k])

            @pl.when(c == 1)
            def _():
                take(full.at[0, 0, :, 0], far_r.at[0, k])

            give(0, k)

    def send_pre(k):
        put(pre, preb.at[y * NX + x], other(k), pre_s, pre_r, tokens)

    def rows_send():
        for b, s in ((0, 2), (1, 0)):

            @pl.when(y == s)
            def _():
                def send(k):
                    py = lax.rem(y + k, NY)
                    remote(xin.at[py, half_rows, :], xi.at[b], xi_s.at[b], xi_r.at[b], (py, dp, c)).start()

                loop(1, NY, send)

    to_row = lax.broadcasted_iota(jnp.int32, (PACK, NX * PAD), 0)
    from_row = lax.broadcasted_iota(jnp.int32, (PACK, NX * PAD), 1)
    from_block = lax.shift_right_logical(from_row, 6)
    inside = from_row - from_block * PAD
    picks = (inside < OWN) & (from_block * OWN + inside == to_row)
    pick = jnp.where(picks, 1.0, 0.0).astype(bf16)

    def pack(s):
        blocks = wx[s * NX : (s + 1) * NX].reshape(NX * PAD, WIDE)
        wg[s, z] = jnp.dot(pick, blocks, preferred_element_type=f32).astype(bf16)
        show(s, z)

    def show(s, chunk):
        remote(wg.at[s, chunk], wsib.at[s, chunk], ws_s.at[s], ws_r.at[s], sibling).start()

    def sibling_weight(s):
        take(wsib.at[s], ws_r.at[s])

    def zag_block(s, chunk, d, k):
        if k == 4:
            return wg.at[s, chunk, :, pl.ds(d * LANE, LANE)]
        return wg.at[s, chunk]

    def zag_take(s, k):
        for d, chunk in ((0, lax.rem(z - k + NZ, NZ)), (1, lax.rem(z + k, NZ))):
            take(zag_block(s, chunk, d, k), zag_r.at[s, d, k - 1])
            if k < 4 or d == 1:
                show(s, chunk)

    def zag(s, k):
        if k > 1:
            zag_take(s, k - 1)
        for d, chunk, where in (
            (0, lax.rem(z - k + 1 + NZ, NZ), up_z),
            (1, lax.rem(z + k - 1, NZ), down_z),
        ):
            block = zag_block(s, chunk, d, k)
            remote(block, block, zag_s.at[s, d, k - 1], zag_r.at[s, d, k - 1], where).start()

    def zrs(s, k):
        ways = ((0, lax.rem(z + 5 - k + NZ, NZ), up_z), (1, lax.rem(z - 5 + k + NZ, NZ), down_z))
        for d, chunk, where in ways:
            rows = pl.ds(pl.multiple_of(chunk * PACK, HALF), PACK)
            side = pl.ds(d * LANE, LANE)
            if k == 1:
                zs[s, d, 0, :, side] = dwp[s, rows, side].astype(bf16)
                src, dst = zs.at[s, d, 0, :, side], zr.at[s, d, 0, :, side]
            else:
                if k == 2:
                    take(zr.at[s, d, 0, :, side], zrs_r.at[s, d, 0])
                    there = pl.ds((1 - d) * LANE, LANE)
                    zs[s, d, 1, :, side] = (dwp[s, rows, side] + zr[s, d, 0, :, side].astype(f32)).astype(bf16)
                    zs[s, d, 1, :, there] = dwp[s, rows, there].astype(bf16)
                else:
                    take(zr.at[s, d, k - 2], zrs_r.at[s, d, k - 2])
                    zs[s, d, k - 1] = (dwp[s, rows, :] + zr[s, d, k - 2].astype(f32)).astype(bf16)
                src, dst = zs.at[s, d, k - 1], zr.at[s, d, k - 1]
            remote(src, dst, zrs_s.at[s, d, k - 1], zrs_r.at[s, d, k - 1], where).start()

    def zrs_finish(s):
        for d in range(2):
            take(zr.at[s, d, 3], zrs_r.at[s, d, 3])
        rows = pl.ds(pl.multiple_of(z * PACK, HALF), PACK)
        total = dwp[s, rows, :] + zr[s, 0, 3].astype(f32) + zr[s, 1, 3].astype(f32)
        spread = lax.dot_general(pick, total.astype(bf16), (((0,), (0,)), ((), ())), preferred_element_type=f32)
        outs[s * NX : (s + 1) * NX] = spread.astype(bf16).reshape(NX, PAD, WIDE)

        def send(px):
            mine = (y == s) & (px == x)

            @pl.when(mine)
            def _():
                outr[gid] = outs[s * NX + px]

            where = (s, z * NX + px, c)

            @pl.when(jnp.logical_not(mine) & slim)
            def _():
                src, dst = outs.at[s * NX + px, :, upper], outr.at[gid, :, upper]
                remote(src, dst, out_s, out_r.at[1], where).start()

            @pl.when(jnp.logical_not(mine) & broad)
            def _():
                remote(outs.at[s * NX + px], outr.at[gid], out_s, out_r.at[0], where).start()

        loop(0, NX, send)

    def unit_rows(b):
        values = xi[b].astype(f32)
        center = values - jnp.mean(values, axis=-1, keepdims=True)
        inv_std = lax.rsqrt(jnp.mean(center * center, axis=-1, keepdims=True) + norm_eps)
        return center * inv_std, inv_std

    def norm_rows(b, s):
        @pl.when(y != s)
        def _():
            take(xi.at[b], xi_r.at[b])

        unit, inv_std = unit_rows(b)
        full[1 + 2 * b, x, y, c] = (unit * scl[s]).astype(bf16)

    def scale_rows(i, s, half):
        def one(p):
            rows = full[2 * i, lax.div(p, NY), lax.rem(p, NY), half].astype(f32) * scl[s]
            scaled[i, p, half] = rows.astype(bf16)

        loop(0, GROUP, one)

    def value_rows(b, s):
        def one(p):
            at = pl.ds(pl.multiple_of(p * ROWS, ROWS), ROWS)
            rows = preb[s * NX + lax.div(p, NY), lax.rem(p, NY)].reshape(ROWS, WIDE)
            act[b, at, :] = gelu_value(rows.astype(f32)).astype(bf16)

        loop(0, GROUP, one)

    def slope_rows(b, s):
        def one(p):
            at = pl.ds(pl.multiple_of(p * HALF, HALF), HALF)
            slope[b, 0, at, :] = gelu_slope(preb[s * NX + lax.div(p, NY), lax.rem(p, NY), c].astype(f32))

        loop(0, GROUP, one)
        take(psib.at[b], ps_r.at[b])

        def two(p):
            at = pl.ds(pl.multiple_of(p * HALF, HALF), HALF)
            slope[b, 1, at, :] = gelu_slope(psib[b, lax.div(p, NY), lax.rem(p, NY)].astype(f32))

        loop(0, GROUP, two)

    def hidden_back(b, down):
        left = scaled[b, :, c].reshape(WIDE, D)
        theirs = jnp.dot(left, wsib[down].reshape(D, WIDE), preferred_element_type=f32).astype(bf16)
        asib[b] = (theirs.astype(f32) * slope[b, 1]).astype(bf16).reshape(GROUP, HALF, WIDE)
        remote(asib.at[b], agrad.at[b, :, c], as_s.at[b], as_r.at[b], sibling).start()
        ours = jnp.dot(left, wg[down].reshape(D, WIDE), preferred_element_type=f32).astype(bf16)
        agrad[b, :, c] = (ours.astype(f32) * slope[b, 0]).astype(bf16).reshape(GROUP, HALF, WIDE)

    def norm_part(b, up):
        dims = (((1,), (1,)), ((), ()))
        ours = agrad[b, :, c].reshape(WIDE, WIDE)
        theirs = asib[b].reshape(WIDE, WIDE)
        product = lax.dot_general(ours, wg[up].reshape(D, WIDE), dims, preferred_element_type=f32)
        product += lax.dot_general(theirs, wsib[up].reshape(D, WIDE), dims, preferred_element_type=f32)
        part[...] = product.reshape(GROUP, HALF, D)

        def one(k):
            p = other(k)
            rss[b, p] = part[p].astype(bf16)
            remote(rss.at[b, p], rsr.at[b, gid], rs_s.at[b], rs_r.at[b], place(p)).start()

        loop(1, GROUP, one)

    def rs_finish(b, s):
        take(rsr.at[b, pl.ds(0, GROUP - 1)], rs_r.at[b])
        total = part[gid]

        def add(k, so_far):
            return so_far + rsr[b, other(k)].astype(f32)

        total = lax.fori_loop(1, GROUP, add, total)
        unit, inv_std = unit_rows(b)
        back = total * scl[s]
        back = inv_std * (
            back
            - jnp.mean(back, axis=-1, keepdims=True)
            - unit * jnp.mean(back * unit, axis=-1, keepdims=True)
        )
        return (full[2 * b, x, y, c].astype(f32) + back).astype(bf16)

    def gradient_in(b):
        take(agrad.at[b, :, oc], as_r.at[b])
        return agrad[b].reshape(TOK, WIDE)

    def weight_part(s, left_ref, right, lead):
        for low, size in ((0, 512), (512, 512), (1024, 640)):
            left = left_ref[lead + (slice(low, low + size),)].reshape(TOK, size)
            dwp[s, low : low + size, :] = lax.dot_general(
                left, right, (((0,), (0,)), ((), ())), preferred_element_type=f32
            )

    def last_rows():
        last = rs_finish(1, 0)

        g0s[...] = last
        remote(g0s, g0f.at[y * 2 + c], g0_s, g0_r, (0, dp, oc)).start()

        @pl.when(y == 0)
        def _():
            g0f[c] = last

        @pl.when(y != 0)
        def _():
            remote(g0s, g0f.at[y * 2 + c], g0_s, g0_r, (0, dp, c)).start()

    def rows_out():
        @pl.when(y == 0)
        def _():
            take(g0f.at[pl.ds(0, 7)], g0_r)
            gout[...] = g0f[...].reshape(NY * ROWS, D)

        @pl.when((y == 1) | (y == 2))
        def _():
            gout[...] = full[2, x].reshape(NY * ROWS, D)

        @pl.when(y == 3)
        def _():
            gout[...] = full[0, x].reshape(NY * ROWS, D)

    def first_drain():
        take_mixed(wx, wx_s, one_dim)
        take_mixed(preb, pre_s, tokens)
        take(scl.at[pl.ds(0, NY - 1)], sc_s)
        for b, s in ((0, 2), (1, 0)):

            @pl.when(y == s)
            def _():
                take(full.at[0, 0, pl.ds(0, NY - 1), 0], xi_s.at[b])

        for i in range(4):
            for k in range(1, NX):
                if i > 0:
                    take(full.at[i, 0, 0, 0], ag_s.at[i, k])
                    take(full.at[i, 0, :, 0], far_s.at[i, k])
            for k in range(NX):
                take(full.at[i, 0, :, 0], sib_s.at[i, k])
        for k in range(1, NX):

            @pl.when(c == 0)
            def _():
                take(full.at[0, 0, 0, 0], ag_s.at[0, k])
                take(full.at[0, 0, pl.ds(0, 3), 0], far_s.at[0, k])

            @pl.when(c == 1)
            def _():
                take(full.at[0, 0, :, 0], far_s.at[0, k])

        for s in range(SECTIONS):
            take(wsib.at[s], ws_s.at[s])
            for d in range(2):
                for k in range(1, 5):
                    take(zag_block(s, 0, d, k), zag_s.at[s, d, k - 1])

    def rs_drain(b):
        take(rss.at[b, pl.ds(0, GROUP - 1)], rs_s.at[b])
        take(asib.at[b], as_s.at[b])
        take(psib.at[b], ps_s.at[b])

    def zrs_drain(s):
        for d in range(2):
            take(zs.at[s, d, 0, :, pl.ds(d * LANE, LANE)], zrs_s.at[s, d, 0])
            for k in range(2, 5):
                take(zs.at[s, d, k - 1], zrs_s.at[s, d, k - 1])

    def weights_in():
        take_pieces(wx, 0, GROUP - 1, wx_r, one_dim)
        take_pieces(wx, 0, 1, local_sem.at[0], one_dim)

    def pre_in():
        take_pieces(preb, 0, GROUP - 1, pre_r, tokens)
        take_pieces(preb, 0, 1, local_sem.at[1], tokens)
        for b, s in ((0, 2), (1, 0)):
            block = preb.at[pl.ds(s * NX, NX), :, oc]
            remote(block, psib.at[b], ps_s.at[b], ps_r.at[b], sibling).start()

    top_send()
    rows_send()
    weights_in()
    pack(3)
    zag(3, 1)
    pack(2)
    zag(2, 1)
    top_spread()
    loop(1, GROUP, send_pre)
    pack(1)
    pack(0)
    take(scl.at[pl.ds(0, NY - 1)], sc_r)
    norm_rows(0, 2)
    norm_rows(1, 0)
    ag_near(1)
    ag_near(3)
    zag(3, 2)
    zag(2, 2)
    zag(3, 3)
    zag(2, 3)
    zag(1, 1)
    top_forward()
    scale_rows(0, 3, c)
    zag(3, 4)
    zag(2, 4)
    zag(0, 1)
    pre_in()
    ag_far(1)
    slope_rows(0, 2)
    zag_take(3, 4)
    sibling_weight(3)
    hidden_back(0, 3)
    zag_take(2, 4)
    sibling_weight(2)
    norm_part(0, 2)
    zag(1, 2)
    ag_finish(0)
    scale_rows(0, 3, oc)
    value_rows(0, 3)
    weight_part(3, scaled.at[0], act[0], tokens)
    zrs(3, 1)
    zag(0, 2)
    value_rows(1, 1)
    slope_rows(1, 0)
    ag_forward(1)
    zag(1, 3)
    zag(0, 3)
    ag_finish(1)
    weight_part(2, full.at[1], gradient_in(0), every)
    zrs(2, 1)
    zrs(3, 2)
    zag(1, 4)
    full[2, x, y, c] = rs_finish(0, 2)
    ag_send(2)
    ag_far(3)
    zag(0, 4)
    ag_spread(2)
    zrs(3, 3)
    zrs(2, 2)
    ag_forward(3)
    ag_forward(2)
    zrs(3, 4)
    scale_rows(1, 1, c)
    zag_take(1, 4)
    sibling_weight(1)
    hidden_back(1, 1)
    zrs(2, 3)
    zag_take(0, 4)
    sibling_weight(0)
    norm_part(1, 0)
    ag_finish(2)
    scale_rows(1, 1, oc)
    weight_part(1, scaled.at[1], act[1], tokens)
    zrs(1, 1)
    zrs(2, 4)
    ag_finish(3)
    weight_part(0, full.at[3], gradient_in(1), every)
    zrs(0, 1)
    zrs(1, 2)
    zrs(0, 2)
    zrs_finish(3)
    first_drain()
    zrs(1, 3)
    zrs(0, 3)
    zrs_finish(2)
    rs_drain(0)
    last_rows()
    zrs(1, 4)
    zrs(0, 4)
    zrs_drain(3)
    zrs_drain(2)
    rs_drain(1)
    zrs_finish(1)
    zrs_finish(0)
    rows_out()
    zrs_drain(1)
    zrs_drain(0)
    take_mixed(outr, out_r, one_dim)
    for p in range(GROUP):
        skip = LANE if p % 2 == 1 and p < 14 else 0
        low = first_block(p) * LANE
        wout[:, low + skip : low + WIDE] = outr[p, :OWN, skip:]
    take_pieces(outs, 0, GROUP - 1, out_s, one_dim)

    @pl.when(y == 0)
    def _():
        take(g0s, g0_s)

    @pl.when(y != 0)
    def _():
        take(g0f.at[pl.ds(0, 2)], g0_s)


def body(llm_grad, slot_row, counts, saved_in, saved_pre, weights, channel_scale):
    hidden = saved_pre.shape[3]
    pre = saved_pre.reshape(NY, 2, HALF, hidden)
    vmem = pl.BlockSpec(memory_space=pltpu.VMEM)
    anywhere = pl.BlockSpec(memory_space=pl.ANY)
    dma = pltpu.SemaphoreType.DMA
    scratch = [
        pltpu.VMEM((PAD, BLOCKS * LANE), bf16),
        pltpu.VMEM((GROUP, PAD, WIDE), bf16),
        pltpu.VMEM((SECTIONS, NZ, PACK, WIDE), bf16),
        pltpu.VMEM((GROUP, NY, 2, HALF, WIDE), bf16),
        pltpu.VMEM((4, NX, NY, 2, HALF, D), bf16),
        pltpu.VMEM((2, GROUP, 2, HALF, D), bf16),
        pltpu.VMEM((GROUP, HALF, D), f32),
        pltpu.VMEM((SECTIONS, NZ, PACK, WIDE), bf16),
        pltpu.VMEM((2, NX, NY, HALF, WIDE), bf16),
        pltpu.VMEM((2, GROUP, HALF, WIDE), bf16),
        pltpu.VMEM((2, GROUP, HALF, D), bf16),
        pltpu.VMEM((2, GROUP, HALF, D), bf16),
        pltpu.VMEM((2, TOK, WIDE), bf16),
        pltpu.VMEM((2, 2, WIDE, WIDE), f32),
        pltpu.VMEM((2, GROUP, 2, HALF, WIDE), bf16),
        pltpu.VMEM((SECTIONS, D, WIDE), f32),
        pltpu.VMEM((SECTIONS, 2, 4, PACK, WIDE), bf16),
        pltpu.VMEM((SECTIONS, 2, 4, PACK, WIDE), bf16),
        pltpu.VMEM((GROUP, PAD, WIDE), bf16),
        pltpu.VMEM((GROUP, PAD, WIDE), bf16),
        pltpu.VMEM((SECTIONS, 1, D), f32),
        pltpu.VMEM((2, HALF, D), bf16),
        pltpu.VMEM((NY * 2, HALF, D), bf16),
        pltpu.VMEM((HALF, D), bf16),
        dma((2,)), dma((2,)), dma, dma((2,)), dma, dma, dma, dma((2,)), dma((2,)),
        dma((4, 4)), dma((4, 4)), dma((4, 4)), dma((4, 4)), dma((4, 4)), dma((4, 4)), dma((4,)), dma((4,)), dma((2,)), dma((2,)), dma((2,)), dma((2,)), dma((2,)), dma((2,)),
        dma((4, 2, 4)), dma((4, 2, 4)), dma((4, 2, 4)), dma((4, 2, 4)), dma, dma((2,)), dma, dma,
    ]
    wout, gout = pl.pallas_call(
        kernel,
        out_shape=(
            jax.ShapeDtypeStruct((OWN, hidden), bf16),
            jax.ShapeDtypeStruct((NY * ROWS, D), bf16),
        ),
        in_specs=[vmem, vmem, pl.BlockSpec(memory_space=pltpu.SMEM), vmem, anywhere, vmem, vmem],
        out_specs=(vmem, vmem),
        scratch_shapes=scratch,
        compiler_params=pltpu.CompilerParams(
            collective_id=0, has_side_effects=True, vmem_limit_bytes=60 * 1024 * 1024
        ),
    )(llm_grad, slot_row[:, 0], counts, saved_in[0], pre, weights[0], channel_scale)
    return (wout[None], gout.reshape(1, NY, ROWS, D))


def solution(mesh):
    in_specs = (
        P(None, "dp", None),
        P(None, "dp", None),
        P("dp", None),
        P("pipe", None, "dp", None),
        P("pipe", None, "dp", "tensor"),
        P("pipe", "dp", "tensor"),
        P("pipe", None),
    )
    out_specs = (P("pipe", "dp", "tensor"), P("pipe", None, "dp", None))
    return jax.shard_map(body, mesh=mesh, in_specs=in_specs, out_specs=out_specs, check_vma=False)
```

```python
import functools

import jax
import jax.numpy as jnp
from jax import lax
from jax.experimental import pallas as pl
from jax.experimental.pallas import tpu as pltpu
from jax.sharding import PartitionSpec as P

norm_eps = 1e-06
root_half = 0.7071067811865476
inv_root_two_pi = 0.3989422804014327

MESH = pl.DeviceIdType.MESH
f32 = jnp.float32
bf16 = jnp.bfloat16

NX, NY, NZ = 4, 4, 8
GROUP = NX * NY
D = 1664
ROWS = 32
HALF = 16
TOK = 512
OWN = 52
PAD = 64
PACK = NX * OWN
LANE = 128
WIDE = 256
BLOCKS = 25
SECTIONS = 4


def first_block(piece):
    return (23 * piece) // 15


def gelu_value(p):
    return p * (0.5 * (1.0 + lax.erf(p * root_half)))


def gelu_slope(p):
    cdf = 0.5 * (1.0 + lax.erf(p * root_half))
    return cdf + p * (jnp.exp(-0.5 * p * p) * inv_root_two_pi)


def kernel(
    llm, slots, counts, xin, pre, w, scale,
    wout, gout,
    wpad, wx, wg, preb, full, scaled, part, wsib, psib, asib, rss, rsr, act, slope, agrad,
    dwp, zs, zr, outs, outr, scl, xi, g0f, g0s,
    local_sem, wx_s, wx_r, pre_s, pre_r, sc_s, sc_r, xi_s, xi_r,
    ag_s, ag_r, far_s, far_r, sib_s, sib_r, ws_s, ws_r, ps_s, ps_r, as_s, as_r, rs_s, rs_r,
    zag_s, zag_r, zrs_s, zrs_r, out_s, out_r, g0_s, g0_r,
):
    y = lax.axis_index("pipe")
    dp = lax.axis_index("dp")
    c = lax.axis_index("tensor")
    z = lax.div(dp, NX)
    x = lax.rem(dp, NX)
    gid = x * NY + y
    oc = 1 - c
    sibling = (y, dp, oc)
    up_z = (y, lax.rem(z + 1, NZ) * NX + x, c)
    down_z = (y, lax.rem(z + NZ - 1, NZ) * NX + x, c)

    def place(piece):
        return (lax.rem(piece, NY), z * NX + lax.div(piece, NY), c)

    def other(k):
        return lax.rem(gid + k, GROUP)

    def loop(low, high, body):
        def step(k, carry):
            body(k)
            return carry

        lax.fori_loop(low, high, step, 0)

    def remote(src, dst, send, recv, where):
        return pltpu.make_async_remote_copy(
            src_ref=src, dst_ref=dst, send_sem=send, recv_sem=recv, device_id=where, device_id_type=MESH
        )

    def take(ref, sem):
        pltpu.make_async_copy(ref, ref, sem).wait()

    def is_narrow(piece):
        return (lax.rem(piece, 2) == 1) & (piece < 14)

    slim = is_narrow(gid)
    broad = jnp.logical_not(slim)
    upper = pl.ds(LANE, LANE)
    one_dim = (slice(None),)
    tokens = (slice(None), slice(None), slice(None))
    every = tokens + one_dim

    def put(src, dst, piece, send, recv, lead):
        low = lax.div(23 * piece, 15) * LANE

        @pl.when(is_narrow(piece))
        def _():
            part_src = src.at[lead + (pl.ds(pl.multiple_of(low + LANE, LANE), LANE),)]
            remote(part_src, dst.at[lead + (upper,)], send.at[1], recv, place(piece)).start()

        @pl.when(jnp.logical_not(is_narrow(piece)))
        def _():
            part_src = src.at[lead + (pl.ds(pl.multiple_of(low, LANE), WIDE),)]
            remote(part_src, dst, send.at[0], recv, place(piece)).start()

    def keep_own(src, dst, sem, lead):
        low = lax.div(23 * gid, 15) * LANE

        @pl.when(slim)
        def _():
            part_src = src.at[lead + (pl.ds(pl.multiple_of(low + LANE, LANE), LANE),)]
            pltpu.make_async_copy(part_src, dst.at[lead + (upper,)], sem).start()

        @pl.when(broad)
        def _():
            part_src = src.at[lead + (pl.ds(pl.multiple_of(low, LANE), WIDE),)]
            pltpu.make_async_copy(part_src, dst, sem).start()

    def take_pieces(ref, low, size, sem, lead):
        @pl.when(slim)
        def _():
            take(ref.at[(pl.ds(low, size),) + lead + (upper,)], sem)

        @pl.when(broad)
        def _():
            take(ref.at[pl.ds(low, size)], sem)

    def take_mixed(ref, sem, lead):
        @pl.when(slim)
        def _():
            take(ref.at[pl.ds(0, 9)], sem.at[0])
            take(ref.at[(pl.ds(0, 6),) + lead + (upper,)], sem.at[1])

        @pl.when(broad)
        def _():
            take(ref.at[pl.ds(0, 8)], sem.at[0])
            take(ref.at[(pl.ds(0, 7),) + lead + (upper,)], sem.at[1])

    barrier = pltpu.get_barrier_semaphore()

    def greet(k):
        pl.semaphore_signal(barrier, inc=1, device_id=place(other(k)), device_id_type=MESH)

    loop(1, GROUP, greet)
    for where in (sibling, up_z, down_z):
        pl.semaphore_signal(barrier, inc=1, device_id=where, device_id_type=MESH)
    def greet_across(k):
        where = (lax.rem(y + k, NY), dp, oc)
        pl.semaphore_signal(barrier, inc=1, device_id=where, device_id_type=MESH)

    loop(1, NY, greet_across)
    keep_own(pre, preb.at[y * NX + x], local_sem.at[1], tokens)

    @pl.when(slim)
    def _():
        wx[:, :, :LANE] = jnp.zeros((GROUP, PAD, LANE), bf16)
        preb[:, :, :, :, :LANE] = jnp.zeros((GROUP, NY, 2, HALF, LANE), bf16)

    wpad[:OWN, :] = w[...]
    wpad[OWN:, :] = jnp.zeros((PAD - OWN, BLOCKS * LANE), bf16)
    keep_own(wpad, wx.at[y * NX + x], local_sem.at[0], one_dim)
    scl[y] = scale[...]
    half_rows = pl.ds(pl.multiple_of(c * HALF, HALF), HALF)
    row_ids = lax.broadcasted_iota(jnp.int32, (HALF, ROWS), 0) + c * HALF
    slot_ids = lax.broadcasted_iota(jnp.int32, (HALF, ROWS), 1)
    for m in range(NY):
        hit = (slots[m : m + 1, :] == row_ids) & (slot_ids < counts[0, m])
        onehot = jnp.where(hit, 1.0, 0.0).astype(bf16)
        full[0, x, m, c] = jnp.dot(onehot, llm[m], preferred_element_type=f32).astype(bf16)
    for b, s in ((0, 2), (1, 0)):

        @pl.when(y == s)
        def _():
            xi[b] = xin[y, half_rows, :]

    pl.semaphore_wait(barrier, GROUP + NY + 1)

    def send_w(k):
        put(wpad, wx.at[y * NX + x], other(k), wx_s, wx_r, one_dim)

    loop(1, GROUP, send_w)

    def send_scale(k):
        py = lax.rem(y + k, NY)
        remote(scale, scl.at[y], sc_s, sc_r, (py, dp, c)).start()

    loop(1, NY, send_scale)

    def near(k):
        return lax.rem(x + k * (1 - c), NX), lax.rem(y + k * c, NY)

    def far(k):
        return lax.rem(x + k * c, NX), lax.rem(y + k * (1 - c), NY)

    def spread(i, q):
        px, py = near(q)
        piece = full.at[i, px, py, c]

        def send(k):
            fx, fy = far(k)
            remote(piece, piece, far_s.at[i, k], far_r.at[i, NX - k], (fy, z * NX + fx, c)).start()

        loop(1, NX, send)

    def ag_near(i):
        piece = full.at[i, x, y, c]

        def send(k):
            px, py = near(k)
            remote(piece, piece, ag_s.at[i, k], ag_r.at[i, NX - k], (py, z * NX + px, c)).start()

        loop(1, NX, send)

    def ag_send(i):
        ag_near(i)
        spread(i, 0)

    def ag_far(i):
        spread(i, 0)
        ag_spread(i)

    def ag_spread(i):
        for q in (1, 3, 2):
            take(full.at[i, 0, 0, 0], ag_r.at[i, q])
            spread(i, q)
        give(i, 0)

    def give(i, k):
        fx, fy = far(k)

        @pl.when(c == 0)
        def _():
            four = full.at[i, :, fy, 0]
            remote(four, four, sib_s.at[i, k], sib_r.at[i, k], sibling).start()

        @pl.when(c == 1)
        def _():
            four = full.at[i, fx, :, 1]
            remote(four, four, sib_s.at[i, k], sib_r.at[i, k], sibling).start()

    def ag_forward(i):
        for k in (1, 3, 2):
            take(full.at[i, 0, :, 0], far_r.at[i, k])
            give(i, k)

    def ag_finish(i):
        for k in range(NX):
            take(full.at[i, 0, :, 0], sib_r.at[i, k])

    def top_send():
        @pl.when(c == 0)
        def _():
            piece = full.at[0, x, y, 0]

            def send(k):
                px, py = near(k)
                remote(piece, piece, ag_s.at[0, k], ag_r.at[0, NX - k], (py, z * NX + px, c)).start()

            loop(1, NX, send)

        @pl.when(c == 1)
        def _():
            four = full.at[0, x, :, 1]

            def send(k):
                fx, fy = far(k)
                remote(four, four, far_s.at[0, k], far_r.at[0, NX - k], (fy, z * NX + fx, c)).start()

            loop(1, NX, send)
            give(0, 0)

    def top_spread():
        @pl.when(c == 0)
        def _():
            for q in (1, 3, 2):
                take(full.at[0, 0, 0, 0], ag_r.at[0, q])
                spread(0, q)
            give(0, 0)

    def top_forward():
        for k in (1, 3, 2):

            @pl.when(c == 0)
            def _():
                take(full.at[0, 0, pl.ds(0, 3), 0], far_r.at[0, k])

            @pl.when(c == 1)
            def _():
                take(full.at[0, 0, :, 0], far_r.at[0, k])

            give(0, k)

    def send_pre(k):
        put(pre, preb.at[y * NX + x], other(k), pre_s, pre_r, tokens)

    def rows_send():
        for b, s in ((0, 2), (1, 0)):

            @pl.when(y == s)
            def _():
                def send(k):
                    py = lax.rem(y + k, NY)
                    remote(xin.at[py, half_rows, :], xi.at[b], xi_s.at[b], xi_r.at[b], (py, dp, c)).start()

                loop(1, NY, send)

    to_row = lax.broadcasted_iota(jnp.int32, (PACK, NX * PAD), 0)
    from_row = lax.broadcasted_iota(jnp.int32, (PACK, NX * PAD), 1)
    from_block = lax.shift_right_logical(from_row, 6)
    inside = from_row - from_block * PAD
    picks = (inside < OWN) & (from_block * OWN + inside == to_row)
    pick = jnp.where(picks, 1.0, 0.0).astype(bf16)

    def pack(s):
        blocks = wx[s * NX : (s + 1) * NX].reshape(NX * PAD, WIDE)
        wg[s, z] = jnp.dot(pick, blocks, preferred_element_type=f32).astype(bf16)
        show(s, z)

    def show(s, chunk):
        remote(wg.at[s, chunk], wsib.at[s, chunk], ws_s.at[s], ws_r.at[s], sibling).start()

    def sibling_weight(s):
        take(wsib.at[s], ws_r.at[s])

    def zag_block(s, chunk, d, k):
        if k == 4:
            return wg.at[s, chunk, :, pl.ds(d * LANE, LANE)]
        return wg.at[s, chunk]

    def zag_take(s, k):
        for d, chunk in ((0, lax.rem(z - k + NZ, NZ)), (1, lax.rem(z + k, NZ))):
            take(zag_block(s, chunk, d, k), zag_r.at[s, d, k - 1])
            if k < 4 or d == 1:
                show(s, chunk)

    def zag(s, k):
        if k > 1:
            zag_take(s, k - 1)
        for d, chunk, where in (
            (0, lax.rem(z - k + 1 + NZ, NZ), up_z),
            (1, lax.rem(z + k - 1, NZ), down_z),
        ):
            block = zag_block(s, chunk, d, k)
            remote(block, block, zag_s.at[s, d, k - 1], zag_r.at[s, d, k - 1], where).start()

    def zrs(s, k):
        ways = ((0, lax.rem(z + 5 - k + NZ, NZ), up_z), (1, lax.rem(z - 5 + k + NZ, NZ), down_z))
        for d, chunk, where in ways:
            rows = pl.ds(pl.multiple_of(chunk * PACK, HALF), PACK)
            side = pl.ds(d * LANE, LANE)
            if k == 1:
                zs[s, d, 0, :, side] = dwp[s, rows, side].astype(bf16)
                src, dst = zs.at[s, d, 0, :, side], zr.at[s, d, 0, :, side]
            else:
                if k == 2:
                    take(zr.at[s, d, 0, :, side], zrs_r.at[s, d, 0])
                    there = pl.ds((1 - d) * LANE, LANE)
                    zs[s, d, 1, :, side] = (dwp[s, rows, side] + zr[s, d, 0, :, side].astype(f32)).astype(bf16)
                    zs[s, d, 1, :, there] = dwp[s, rows, there].astype(bf16)
                else:
                    take(zr.at[s, d, k - 2], zrs_r.at[s, d, k - 2])
                    zs[s, d, k - 1] = (dwp[s, rows, :] + zr[s, d, k - 2].astype(f32)).astype(bf16)
                src, dst = zs.at[s, d, k - 1], zr.at[s, d, k - 1]
            remote(src, dst, zrs_s.at[s, d, k - 1], zrs_r.at[s, d, k - 1], where).start()

    def zrs_finish(s):
        for d in range(2):
            take(zr.at[s, d, 3], zrs_r.at[s, d, 3])
        rows = pl.ds(pl.multiple_of(z * PACK, HALF), PACK)
        total = dwp[s, rows, :] + zr[s, 0, 3].astype(f32) + zr[s, 1, 3].astype(f32)
        spread = lax.dot_general(pick, total.astype(bf16), (((0,), (0,)), ((), ())), preferred_element_type=f32)
        outs[s * NX : (s + 1) * NX] = spread.astype(bf16).reshape(NX, PAD, WIDE)

        def send(px):
            mine = (y == s) & (px == x)

            @pl.when(mine)
            def _():
                outr[gid] = outs[s * NX + px]

            where = (s, z * NX + px, c)

            @pl.when(jnp.logical_not(mine) & slim)
            def _():
                src, dst = outs.at[s * NX + px, :, upper], outr.at[gid, :, upper]
                remote(src, dst, out_s, out_r.at[1], where).start()

            @pl.when(jnp.logical_not(mine) & broad)
            def _():
                remote(outs.at[s * NX + px], outr.at[gid], out_s, out_r.at[0], where).start()

        loop(0, NX, send)

    def unit_rows(b):
        values = xi[b].astype(f32)
        center = values - jnp.mean(values, axis=-1, keepdims=True)
        inv_std = lax.rsqrt(jnp.mean(center * center, axis=-1, keepdims=True) + norm_eps)
        return center * inv_std, inv_std

    def norm_rows(b, s):
        @pl.when(y != s)
        def _():
            take(xi.at[b], xi_r.at[b])

        unit, inv_std = unit_rows(b)
        full[1 + 2 * b, x, y, c] = (unit * scl[s]).astype(bf16)

    def scale_rows(i, s, half):
        def one(p):
            rows = full[2 * i, lax.div(p, NY), lax.rem(p, NY), half].astype(f32) * scl[s]
            scaled[i, p, half] = rows.astype(bf16)

        loop(0, GROUP, one)

    def value_rows(b, s):
        def one(p):
            at = pl.ds(pl.multiple_of(p * ROWS, ROWS), ROWS)
            rows = preb[s * NX + lax.div(p, NY), lax.rem(p, NY)].reshape(ROWS, WIDE)
            act[b, at, :] = gelu_value(rows.astype(f32)).astype(bf16)

        loop(0, GROUP, one)

    def slope_rows(b, s):
        def one(p):
            at = pl.ds(pl.multiple_of(p * HALF, HALF), HALF)
            slope[b, 0, at, :] = gelu_slope(preb[s * NX + lax.div(p, NY), lax.rem(p, NY), c].astype(f32))

        loop(0, GROUP, one)
        take(psib.at[b], ps_r.at[b])

        def two(p):
            at = pl.ds(pl.multiple_of(p * HALF, HALF), HALF)
            slope[b, 1, at, :] = gelu_slope(psib[b, lax.div(p, NY), lax.rem(p, NY)].astype(f32))

        loop(0, GROUP, two)

    def hidden_back(b, down):
        left = scaled[b, :, c].reshape(WIDE, D)
        theirs = jnp.dot(left, wsib[down].reshape(D, WIDE), preferred_element_type=f32).astype(bf16)
        asib[b] = (theirs.astype(f32) * slope[b, 1]).astype(bf16).reshape(GROUP, HALF, WIDE)
        remote(asib.at[b], agrad.at[b, :, c], as_s.at[b], as_r.at[b], sibling).start()
        ours = jnp.dot(left, wg[down].reshape(D, WIDE), preferred_element_type=f32).astype(bf16)
        agrad[b, :, c] = (ours.astype(f32) * slope[b, 0]).astype(bf16).reshape(GROUP, HALF, WIDE)

    def norm_part(b, up):
        dims = (((1,), (1,)), ((), ()))
        ours = agrad[b, :, c].reshape(WIDE, WIDE)
        theirs = asib[b].reshape(WIDE, WIDE)
        product = lax.dot_general(ours, wg[up].reshape(D, WIDE), dims, preferred_element_type=f32)
        product += lax.dot_general(theirs, wsib[up].reshape(D, WIDE), dims, preferred_element_type=f32)
        part[...] = product.reshape(GROUP, HALF, D)

        def one(k):
            p = other(k)
            rss[b, p] = part[p].astype(bf16)
            remote(rss.at[b, p], rsr.at[b, gid], rs_s.at[b], rs_r.at[b], place(p)).start()

        loop(1, GROUP, one)

    def rs_finish(b, s):
        take(rsr.at[b, pl.ds(0, GROUP - 1)], rs_r.at[b])
        total = part[gid]

        def add(k, so_far):
            return so_far + rsr[b, other(k)].astype(f32)

        total = lax.fori_loop(1, GROUP, add, total)
        unit, inv_std = unit_rows(b)
        back = total * scl[s]
        back = inv_std * (
            back
            - jnp.mean(back, axis=-1, keepdims=True)
            - unit * jnp.mean(back * unit, axis=-1, keepdims=True)
        )
        return (full[2 * b, x, y, c].astype(f32) + back).astype(bf16)

    def gradient_in(b):
        take(agrad.at[b, :, oc], as_r.at[b])
        return agrad[b].reshape(TOK, WIDE)

    def weight_part(s, left_ref, right, lead):
        for low, size in ((0, 512), (512, 512), (1024, 640)):
            left = left_ref[lead + (slice(low, low + size),)].reshape(TOK, size)
            dwp[s, low : low + size, :] = lax.dot_general(
                left, right, (((0,), (0,)), ((), ())), preferred_element_type=f32
            )

    def last_rows():
        last = rs_finish(1, 0)

        g0s[...] = last
        remote(g0s, g0f.at[y * 2 + c], g0_s, g0_r, (0, dp, oc)).start()

        @pl.when(y == 0)
        def _():
            g0f[c] = last

        @pl.when(y != 0)
        def _():
            remote(g0s, g0f.at[y * 2 + c], g0_s, g0_r, (0, dp, c)).start()

    def rows_out():
        @pl.when(y == 0)
        def _():
            take(g0f.at[pl.ds(0, 7)], g0_r)
            gout[...] = g0f[...].reshape(NY * ROWS, D)

        @pl.when((y == 1) | (y == 2))
        def _():
            gout[...] = full[2, x].reshape(NY * ROWS, D)

        @pl.when(y == 3)
        def _():
            gout[...] = full[0, x].reshape(NY * ROWS, D)

    def first_drain():
        take_mixed(wx, wx_s, one_dim)
        take_mixed(preb, pre_s, tokens)
        take(scl.at[pl.ds(0, NY - 1)], sc_s)
        for b, s in ((0, 2), (1, 0)):

            @pl.when(y == s)
            def _():
                take(full.at[0, 0, pl.ds(0, NY - 1), 0], xi_s.at[b])

        for i in range(4):
            for k in range(1, NX):
                if i > 0:
                    take(full.at[i, 0, 0, 0], ag_s.at[i, k])
                    take(full.at[i, 0, :, 0], far_s.at[i, k])
            for k in range(NX):
                take(full.at[i, 0, :, 0], sib_s.at[i, k])
        for k in range(1, NX):

            @pl.when(c == 0)
            def _():
                take(full.at[0, 0, 0, 0], ag_s.at[0, k])
                take(full.at[0, 0, pl.ds(0, 3), 0], far_s.at[0, k])

            @pl.when(c == 1)
            def _():
                take(full.at[0, 0, :, 0], far_s.at[0, k])

        for s in range(SECTIONS):
            take(wsib.at[s], ws_s.at[s])
            for d in range(2):
                for k in range(1, 5):
                    take(zag_block(s, 0, d, k), zag_s.at[s, d, k - 1])

    def rs_drain(b):
        take(rss.at[b, pl.ds(0, GROUP - 1)], rs_s.at[b])
        take(asib.at[b], as_s.at[b])
        take(psib.at[b], ps_s.at[b])

    def zrs_drain(s):
        for d in range(2):
            take(zs.at[s, d, 0, :, pl.ds(d * LANE, LANE)], zrs_s.at[s, d, 0])
            for k in range(2, 5):
                take(zs.at[s, d, k - 1], zrs_s.at[s, d, k - 1])

    def weights_in():
        take_pieces(wx, 0, GROUP - 1, wx_r, one_dim)
        take_pieces(wx, 0, 1, local_sem.at[0], one_dim)

    def pre_in():
        take_pieces(preb, 0, GROUP - 1, pre_r, tokens)
        take_pieces(preb, 0, 1, local_sem.at[1], tokens)
        for b, s in ((0, 2), (1, 0)):
            block = preb.at[pl.ds(s * NX, NX), :, oc]
            remote(block, psib.at[b], ps_s.at[b], ps_r.at[b], sibling).start()

    top_send()
    rows_send()
    loop(1, GROUP, send_pre)
    weights_in()
    pack(3)
    zag(3, 1)
    pack(2)
    zag(2, 1)
    top_spread()
    pack(1)
    pack(0)
    take(scl.at[pl.ds(0, NY - 1)], sc_r)
    norm_rows(0, 2)
    norm_rows(1, 0)
    ag_near(1)
    ag_near(3)
    zag(3, 2)
    zag(2, 2)
    zag(3, 3)
    zag(2, 3)
    zag(1, 1)
    top_forward()
    scale_rows(0, 3, c)
    zag(3, 4)
    zag(2, 4)
    zag(0, 1)
    pre_in()
    ag_far(1)
    slope_rows(0, 2)
    zag_take(3, 4)
    sibling_weight(3)
    hidden_back(0, 3)
    zag_take(2, 4)
    sibling_weight(2)
    norm_part(0, 2)
    zag(1, 2)
    ag_finish(0)
    scale_rows(0, 3, oc)
    value_rows(0, 3)
    weight_part(3, scaled.at[0], act[0], tokens)
    zrs(3, 1)
    zag(0, 2)
    value_rows(1, 1)
    slope_rows(1, 0)
    ag_forward(1)
    zag(1, 3)
    zag(0, 3)
    ag_finish(1)
    weight_part(2, full.at[1], gradient_in(0), every)
    full[2, x, y, c] = rs_finish(0, 2)
    ag_send(2)
    zrs(2, 1)
    zrs(3, 2)
    zag(1, 4)
    ag_far(3)
    zag(0, 4)
    zrs(2, 2)
    ag_spread(2)
    zrs(3, 3)
    ag_forward(3)
    ag_forward(2)
    zrs(3, 4)
    zrs(2, 3)
    scale_rows(1, 1, c)
    zag_take(1, 4)
    sibling_weight(1)
    hidden_back(1, 1)
    zag_take(0, 4)
    sibling_weight(0)
    norm_part(1, 0)
    ag_finish(2)
    scale_rows(1, 1, oc)
    weight_part(1, scaled.at[1], act[1], tokens)
    zrs(1, 1)
    zrs(2, 4)
    ag_finish(3)
    weight_part(0, full.at[3], gradient_in(1), every)
    zrs(0, 1)
    zrs(1, 2)
    zrs(0, 2)
    zrs_finish(3)
    first_drain()
    zrs(1, 3)
    zrs(0, 3)
    zrs_finish(2)
    rs_drain(0)
    last_rows()
    zrs(1, 4)
    zrs(0, 4)
    zrs_drain(3)
    zrs_drain(2)
    rs_drain(1)
    zrs_finish(1)
    zrs_finish(0)
    rows_out()
    zrs_drain(1)
    zrs_drain(0)
    take_mixed(outr, out_r, one_dim)
    for p in range(GROUP):
        skip = LANE if p % 2 == 1 and p < 14 else 0
        low = first_block(p) * LANE
        wout[:, low + skip : low + WIDE] = outr[p, :OWN, skip:]
    take_pieces(outs, 0, GROUP - 1, out_s, one_dim)

    @pl.when(y == 0)
    def _():
        take(g0s, g0_s)

    @pl.when(y != 0)
    def _():
        take(g0f.at[pl.ds(0, 2)], g0_s)


def body(llm_grad, slot_row, counts, saved_in, saved_pre, weights, channel_scale):
    hidden = saved_pre.shape[3]
    pre = saved_pre.reshape(NY, 2, HALF, hidden)
    vmem = pl.BlockSpec(memory_space=pltpu.VMEM)
    anywhere = pl.BlockSpec(memory_space=pl.ANY)
    dma = pltpu.SemaphoreType.DMA
    scratch = [
        pltpu.VMEM((PAD, BLOCKS * LANE), bf16),
        pltpu.VMEM((GROUP, PAD, WIDE), bf16),
        pltpu.VMEM((SECTIONS, NZ, PACK, WIDE), bf16),
        pltpu.VMEM((GROUP, NY, 2, HALF, WIDE), bf16),
        pltpu.VMEM((4, NX, NY, 2, HALF, D), bf16),
        pltpu.VMEM((2, GROUP, 2, HALF, D), bf16),
        pltpu.VMEM((GROUP, HALF, D), f32),
        pltpu.VMEM((SECTIONS, NZ, PACK, WIDE), bf16),
        pltpu.VMEM((2, NX, NY, HALF, WIDE), bf16),
        pltpu.VMEM((2, GROUP, HALF, WIDE), bf16),
        pltpu.VMEM((2, GROUP, HALF, D), bf16),
        pltpu.VMEM((2, GROUP, HALF, D), bf16),
        pltpu.VMEM((2, TOK, WIDE), bf16),
        pltpu.VMEM((2, 2, WIDE, WIDE), f32),
        pltpu.VMEM((2, GROUP, 2, HALF, WIDE), bf16),
        pltpu.VMEM((SECTIONS, D, WIDE), f32),
        pltpu.VMEM((SECTIONS, 2, 4, PACK, WIDE), bf16),
        pltpu.VMEM((SECTIONS, 2, 4, PACK, WIDE), bf16),
        pltpu.VMEM((GROUP, PAD, WIDE), bf16),
        pltpu.VMEM((GROUP, PAD, WIDE), bf16),
        pltpu.VMEM((SECTIONS, 1, D), f32),
        pltpu.VMEM((2, HALF, D), bf16),
        pltpu.VMEM((NY * 2, HALF, D), bf16),
        pltpu.VMEM((HALF, D), bf16),
        dma((2,)), dma((2,)), dma, dma((2,)), dma, dma, dma, dma((2,)), dma((2,)),
        dma((4, 4)), dma((4, 4)), dma((4, 4)), dma((4, 4)), dma((4, 4)), dma((4, 4)), dma((4,)), dma((4,)), dma((2,)), dma((2,)), dma((2,)), dma((2,)), dma((2,)), dma((2,)),
        dma((4, 2, 4)), dma((4, 2, 4)), dma((4, 2, 4)), dma((4, 2, 4)), dma, dma((2,)), dma, dma,
    ]
    wout, gout = pl.pallas_call(
        kernel,
        out_shape=(
            jax.ShapeDtypeStruct((OWN, hidden), bf16),
            jax.ShapeDtypeStruct((NY * ROWS, D), bf16),
        ),
        in_specs=[vmem, vmem, pl.BlockSpec(memory_space=pltpu.SMEM), vmem, anywhere, vmem, vmem],
        out_specs=(vmem, vmem),
        scratch_shapes=scratch,
        compiler_params=pltpu.CompilerParams(
            collective_id=0, has_side_effects=True, vmem_limit_bytes=60 * 1024 * 1024
        ),
    )(llm_grad, slot_row[:, 0], counts, saved_in[0], pre, weights[0], channel_scale)
    return (wout[None], gout.reshape(1, NY, ROWS, D))


def solution(mesh):
    in_specs = (
        P(None, "dp", None),
        P(None, "dp", None),
        P("dp", None),
        P("pipe", None, "dp", None),
        P("pipe", None, "dp", "tensor"),
        P("pipe", "dp", "tensor"),
        P("pipe", None),
    )
    out_specs = (P("pipe", "dp", "tensor"), P("pipe", None, "dp", None))
    return jax.shard_map(body, mesh=mesh, in_specs=in_specs, out_specs=out_specs, check_vma=False)
```
